32 devices in a mesh: rows: 8 (over z, y), pairs: 4 (over x, core).
Axes of the slice: x: 2, y: 2, z: 4, core: 2. Of those that a mesh axis runs over, the one named last changes fastest.
Arguments:
- latent: float32 [16384, 128], P('rows'), may hold values from -2.5 to 2.5
- left_block: int32 [8, 4, 8, 2], P('rows', 'pairs'), may hold values from 0 to 15, as said below
- right_block: int32 [8, 4, 8, 2], P('rows', 'pairs'), may hold values from 0 to 15
- slot_kind: int32 [8, 4, 8, 2], P('rows', 'pairs'), may hold values from 0 to 2, as said below
- edge_cols: int32 [8, 4, 8, 2, 8, 128], P('rows', 'pairs'), may hold values from 0 to 127
Outputs:
- latent_grad: float32 [16384, 128], P(('rows', 'pairs'))
The draws below stay inside these ranges and needn't reach their ends.
Inputs may be any that keep to these rules, and one draw needn't show every extreme that they name: `slot_kind`: exactly the slots whose third index s is lower than the first index r hold 0; every other slot holds 1 or 2. On slots whose third index equals the first, left_block <= right_block, so that every listed pair has its left block at or before its right block.
All inputs are finite; a program needn't handle non-finite values.
Results may differ from the reference program's by a relative error of at most 0.0003.
Values sent between devices are 32-bit elements; how exact they have to be, the bound alone decides.
No kernel may reach another device: no remote copies, remote signals or barrier semaphores. Data moves between devices by JAX's collectives and lax.ppermute only.
A program may use at most 128 MiB of HBM per device.

```python
import jax
import jax.numpy as jnp
from jax import lax

DL = 128
BLOCK = 128
BLK_DEV = 16
CAP = 2
NBR = 8
NODES = 16384
N_ROWS = 8
N_PAIRS = 4


def slot_tables(base_key):
    shape = (N_ROWS, N_PAIRS, N_ROWS, CAP)
    source = lax.broadcasted_iota(jnp.int32, shape, 0)
    destination = lax.broadcasted_iota(jnp.int32, shape, 2)
    first = jax.random.randint(jax.random.fold_in(base_key, 11), shape, 0, BLK_DEV)
    second = jax.random.randint(jax.random.fold_in(base_key, 12), shape, 0, BLK_DEV)
    same = source == destination
    left_ids = jnp.where(same, jnp.minimum(first, second), first)
    right_ids = jnp.where(same, jnp.maximum(first, second), second)
    kinds = jax.random.randint(jax.random.fold_in(base_key, 13), shape, 1, 3)
    kinds = jnp.where(destination >= source, kinds, 0)
    return (left_ids.astype(jnp.int32), right_ids.astype(jnp.int32), kinds.astype(jnp.int32))


def draw_left_block(key, part):
    return slot_tables(key)[0]


def draw_right_block(key, part):
    return slot_tables(key)[1]


def draw_slot_kind(key, part):
    return slot_tables(key)[2]


def draw_edge_cols(key, part):
    shape = (N_ROWS, N_PAIRS, N_ROWS, CAP, NBR, BLOCK)
    return jax.random.randint(jax.random.fold_in(key, 14), shape, 0, BLOCK).astype(jnp.int32)


def level_of(key, dims, cuts, smallest, high):
    factor_of, own = 1.0, jax.random.fold_in(key, 6)
    for position, blocks in cuts:
        steps = jnp.exp(jax.random.uniform(jax.random.fold_in(own, position), (blocks,), jnp.float32, smallest / len(cuts), high / len(cuts)))
        factor_of = factor_of * jnp.repeat(steps, dims[position] // blocks).reshape([-1 if axis == position else 1 for axis in range(len(dims))])
    return factor_of


def scatter_about(own_key, shape, scale, bound, pieces=(), kind=jnp.bfloat16):
    entries = scale * jax.random.normal(own_key, shape, jnp.float32)
    if pieces:
        entries = entries * level_of(own_key, shape, pieces, -0.22, 0.18)
    return jnp.clip(entries, -bound, bound).astype(kind)


def setup_inputs(seed: int = 0) -> dict:
    keys = jax.random.split(jax.random.key(seed), 6)
    latent = scatter_about(keys[0], (NODES, DL), 0.35, 2.5, ((0, 8),), jnp.float32)
    left_block = draw_left_block(jax.random.fold_in(keys[5], 71), 0)
    right_block = draw_right_block(jax.random.fold_in(keys[5], 71), 0)
    slot_kind = draw_slot_kind(jax.random.fold_in(keys[5], 71), 0)
    edge_cols = draw_edge_cols(jax.random.fold_in(keys[5], 71), 0)
    return dict(latent=latent, left_block=left_block, right_block=right_block, slot_kind=slot_kind, edge_cols=edge_cols)


def residual(left_rows, right_rows, slot_kinds, edge_ids):
    scores = jnp.einsum('...id,...jd->...ij', left_rows, right_rows, precision=lax.Precision.HIGHEST)
    columns = lax.broadcasted_iota(jnp.int32, scores.shape, scores.ndim - 1)
    target_hit = jnp.zeros(scores.shape, jnp.bool_)
    for which in range(edge_ids.shape[-2]):
        target_hit = target_hit | (edge_ids[..., which, :, None] == columns)
    positive = (slot_kinds == 2)[..., None, None]
    target = jnp.where(target_hit & positive, jnp.ones_like(scores), jnp.zeros_like(scores))
    live = (slot_kinds > 0)[..., None, None]
    return jnp.where(live, jax.nn.sigmoid(scores) - target, jnp.zeros_like(scores))


def reference(latent, left_block, right_block, slot_kind, edge_cols):
    blocks = latent.reshape(N_ROWS * BLK_DEV, BLOCK, DL)

    def one_source(gradient, source):
        left_ids = left_block[source] + source * BLK_DEV
        destination = lax.broadcasted_iota(jnp.int32, left_ids.shape, 1)
        right_ids = right_block[source] + destination * BLK_DEV
        left_rows = blocks[left_ids]
        right_rows = blocks[right_ids]
        residue = residual(left_rows, right_rows, slot_kind[source], edge_cols[source])
        left_grad = jnp.einsum('...ij,...jd->...id', residue, right_rows, precision=lax.Precision.HIGHEST)
        right_grad = jnp.einsum('...ij,...id->...jd', residue, left_rows, precision=lax.Precision.HIGHEST)
        gradient = gradient.at[left_ids.reshape(-1)].add(left_grad.reshape(-1, BLOCK, DL))
        gradient = gradient.at[right_ids.reshape(-1)].add(right_grad.reshape(-1, BLOCK, DL))
        return gradient, None

    gradient, _ = lax.scan(one_source, jnp.zeros(blocks.shape, latent.dtype), jnp.arange(N_ROWS, dtype=jnp.int32))
    return gradient.reshape(NODES, DL)
```

```python
import functools

import jax
import jax.numpy as jnp
from jax import lax
from jax.experimental import pallas as pl
from jax.experimental.pallas import tpu as pltpu
from jax.sharding import PartitionSpec as P

F32 = jnp.float32
BF16 = jnp.bfloat16
SMEM = pl.BlockSpec(memory_space=pltpu.SMEM)
VMEM = pl.BlockSpec(memory_space=pltpu.VMEM)
PARAMS = pltpu.CompilerParams(vmem_limit_bytes=48 * 1024 * 1024)


def halves(value):
    high = value.astype(BF16)
    return high, (value - high.astype(F32)).astype(BF16)


def product(left, right, dims):
    (a, b), (c, d) = left, right
    one = functools.partial(
        lax.dot_general, dimension_numbers=((dims[:1], dims[1:]), ((), ())), preferred_element_type=F32
    )
    return one(a, c) + (one(a, d) + one(b, c))


def natural_target(edges):
    width = edges.shape[-1]
    row = lax.broadcasted_iota(jnp.int32, (width, width), 0).astype(F32)
    hit = row == edges[0:1, :]
    for which in range(1, edges.shape[0]):
        hit = hit | (row == edges[which : which + 1, :])
    return jnp.where(hit, 1.0, 0.0)


def coded_edges(edges_ref, kind_ref, peer, slot):
    edges = edges_ref[peer, slot].astype(F32)
    return jnp.where(kind_ref[peer, slot] == 2, edges, -1.0)


def own_id(left_ref, asked_ref, me, peer, slot):
    return jnp.where(peer >= me, left_ref[peer, slot], asked_ref[peer, slot])


def pack_kernel(shifts, left_ref, asked_ref, kind_ref, latent_ref, edges_ref, *message_refs):
    me = lax.axis_index("rows")
    tile = latent_ref.shape[1]
    for shift, message_ref in zip(shifts, message_refs):
        peer = me ^ shift
        for slot in range(message_ref.shape[0]):
            block = own_id(left_ref, asked_ref, me, peer, slot)
            message_ref[slot, :tile] = latent_ref[block]
            message_ref[slot, tile:] = coded_edges(edges_ref, kind_ref, peer, slot)


def add_peer(shift, total_ref, left_ref, asked_ref, kind_ref, latent_ref, edges_ref, message_ref):
    me = lax.axis_index("rows")
    peer = me ^ shift
    low = peer > me
    quarter = lax.axis_index("pairs") * (total_ref.shape[0] // lax.axis_size("pairs"))
    tile = latent_ref.shape[1]
    for slot in range(message_ref.shape[0]):
        block = own_id(left_ref, asked_ref, me, peer, slot)
        own = halves(latent_ref[block])
        other = halves(message_ref[slot, :tile])
        sent = message_ref[slot, tile:]
        edges = jnp.where(low, coded_edges(edges_ref, kind_ref, peer, slot), sent)
        target = natural_target(edges)
        target = jnp.where(low, target.T, target)
        residue = jax.nn.sigmoid(product(own, other, (1, 1))) - target
        total_ref[block ^ quarter] += product(halves(residue), other, (1, 0))


def add_own(total_ref, left_ref, right_ref, kind_ref, latent_ref, edges_ref):
    me = lax.axis_index("rows")
    quarter = lax.axis_index("pairs") * (total_ref.shape[0] // lax.axis_size("pairs"))
    for slot in range(edges_ref.shape[1]):
        left_block, right_block = left_ref[me, slot], right_ref[me, slot]
        left, right = halves(latent_ref[left_block]), halves(latent_ref[right_block])
        target = natural_target(coded_edges(edges_ref, kind_ref, me, slot))
        residue = halves(jax.nn.sigmoid(product(right, left, (1, 1))) - target)
        total_ref[left_block ^ quarter] += product(residue, right, (0, 0))
        total_ref[right_block ^ quarter] += product(residue, left, (1, 0))


def first_kernel(shifts, left_ref, right_ref, asked_ref, kind_ref, latent_ref, edges_ref, *refs):
    *message_refs, total_ref = refs
    total_ref[...] = jnp.zeros_like(total_ref)
    add_own(total_ref, left_ref, right_ref, kind_ref, latent_ref, edges_ref)
    for shift, message_ref in zip(shifts, message_refs):
        add_peer(shift, total_ref, left_ref, asked_ref, kind_ref, latent_ref, edges_ref, message_ref)


def last_kernel(shifts, left_ref, asked_ref, kind_ref, latent_ref, edges_ref, before_ref, *refs):
    count = len(shifts)
    message_refs, part_refs, total_ref = refs[:count], refs[count:-1], refs[-1]
    total_ref[...] = before_ref[...]
    for shift, message_ref in zip(shifts, message_refs):
        add_peer(shift, total_ref, left_ref, asked_ref, kind_ref, latent_ref, edges_ref, message_ref)
    depth = part_refs[0].shape[0]
    for place, part_ref in enumerate(part_refs):
        part_ref[...] = total_ref[place * depth : (place + 1) * depth]


def estimate(slots, width, moved):
    return pl.CostEstimate(flops=12 * slots * width**3, bytes_accessed=moved, transcendentals=slots * width**2)


def swap(value, axis, shift):
    return lax.ppermute(value, axis, [(at, at ^ shift) for at in range(lax.axis_size(axis))])


def body(latent, left_block, right_block, slot_kind, edge_cols):
    tile, width = edge_cols.shape[-1], latent.shape[1]
    blocks = latent.reshape(-1, tile, width)
    peers, slots = left_block.shape[2:]
    lists = edge_cols.shape[4]
    left_ids = left_block.reshape(peers, slots)
    right_ids = right_block.reshape(peers, slots)
    kinds = slot_kind.reshape(peers, slots)
    edges = edge_cols.reshape(peers, slots, lists, tile)
    asked = lax.all_to_all(right_ids.reshape(peers, 1, slots), "rows", 0, 0, tiled=True).reshape(peers, slots)

    top = peers // 2
    far, near = tuple(range(top, peers)), tuple(range(1, top))
    order = far + near
    message = jax.ShapeDtypeStruct((slots, tile + lists, width), F32)
    total = jax.ShapeDtypeStruct(blocks.shape, F32)
    messages = pl.pallas_call(
        functools.partial(pack_kernel, order),
        out_shape=[message] * len(order),
        in_specs=[SMEM] * 3 + [VMEM] * 2,
        out_specs=[VMEM] * len(order),
        compiler_params=PARAMS,
    )(left_ids, asked, kinds, blocks, edges)
    arrived = {shift: swap(value, "rows", shift) for shift, value in zip(order, messages)}

    before = pl.pallas_call(
        functools.partial(first_kernel, near),
        out_shape=total,
        in_specs=[SMEM] * 4 + [VMEM] * (2 + len(near)),
        out_specs=VMEM,
        compiler_params=PARAMS,
        cost_estimate=estimate(slots * (1 + len(near)), tile, 2 * blocks.size * 4),
    )(left_ids, right_ids, asked, kinds, blocks, edges, *[arrived[shift] for shift in near])
    parts = lax.axis_size("pairs")
    part = jax.ShapeDtypeStruct((blocks.shape[0] // parts, tile, width), F32)
    held = pl.pallas_call(
        functools.partial(last_kernel, far),
        out_shape=[part] * parts,
        in_specs=[SMEM] * 3 + [VMEM] * (3 + len(far)),
        out_specs=[VMEM] * parts,
        scratch_shapes=[pltpu.VMEM(blocks.shape, F32)],
        compiler_params=PARAMS,
        cost_estimate=estimate(slots * len(far), tile, 3 * blocks.size * 4),
    )(left_ids, asked, kinds, blocks, edges, before, *[arrived[shift] for shift in far])
    far_half = held[2] + swap(held[3], "pairs", 1)
    kept = swap(held[1], "pairs", 1)
    result = held[0] + kept + swap(far_half, "pairs", 2)
    return result.reshape(-1, width)


def solution(mesh):
    return jax.shard_map(
        body,
        mesh=mesh,
        in_specs=(
            P("rows", None),
            P("rows", "pairs", None, None),
            P("rows", "pairs", None, None),
            P("rows", "pairs", None, None),
            P("rows", "pairs", None, None, None, None),
        ),
        out_specs=P(("rows", "pairs"), None),
        check_vma=False,
    )
```

```python
import functools

import jax
import jax.numpy as jnp
from jax import lax
from jax.experimental import pallas as pl
from jax.experimental.pallas import tpu as pltpu
from jax.sharding import PartitionSpec as P

F32 = jnp.float32
BF16 = jnp.bfloat16
SMEM = pl.BlockSpec(memory_space=pltpu.SMEM)
VMEM = pl.BlockSpec(memory_space=pltpu.VMEM)
HBM = pl.BlockSpec(memory_space=pltpu.HBM)
PARAMS = pltpu.CompilerParams(vmem_limit_bytes=16 * 1024 * 1024)


def halves(value):
    high = value.astype(BF16)
    return high, (value - high.astype(F32)).astype(BF16)


def product(left, right, left_dim, right_dim):
    deep = jnp.concatenate(left, left_dim)
    both = [jnp.concatenate([half, half], right_dim) for half in right]
    wide = jnp.concatenate(both, 1 - right_dim)
    sums = lax.dot_general(
        deep, wide, (((left_dim,), (right_dim,)), ((), ())), preferred_element_type=F32
    )
    width = sums.shape[1] // 2
    return sums[:, :width] + sums[:, width:]


def natural_target(edges):
    width = edges.shape[-1]
    row = lax.broadcasted_iota(jnp.int32, (width, width), 0).astype(F32)
    hit = row == edges[0:1, :]
    for which in range(1, edges.shape[0]):
        hit = hit | (row == edges[which : which + 1, :])
    return jnp.where(hit, 1.0, 0.0)


def own_id(ids_ref, asked_ref, place, me, peer, slot):
    return jnp.where(peer > me, ids_ref[0, slot, peer], asked_ref[place, slot, me])


def pack_kernel(shifts, places, ids_ref, asked_ref, latent_ref, coded_ref, *message_refs):
    me = lax.axis_index("rows")
    tile = latent_ref.shape[1]
    for shift, place, message_ref in zip(shifts, places, message_refs):
        peer = me ^ shift
        for slot in range(message_ref.shape[0]):
            block = own_id(ids_ref, asked_ref, place, me, peer, slot)
            message_ref[slot, :tile] = latent_ref[block]
            message_ref[slot, tile:] = coded_ref[peer, slot]


def add_peer(shift, place, total_ref, ids_ref, asked_ref, latent_ref, coded_ref, message_ref):
    me = lax.axis_index("rows")
    peer = me ^ shift
    low = peer > me
    quarter = lax.axis_index("pairs") * (total_ref.shape[0] // lax.axis_size("pairs"))
    tile = latent_ref.shape[1]
    for slot in range(message_ref.shape[0]):
        block = own_id(ids_ref, asked_ref, place, me, peer, slot)
        own = halves(latent_ref[block])
        other = halves(message_ref[slot, :tile])
        edges = jnp.where(low, coded_ref[peer, slot], message_ref[slot, tile:])
        target = natural_target(edges)
        target = jnp.where(low, target.T, target)
        residue = jax.nn.sigmoid(product(own, other, 1, 1)) - target
        total_ref[block ^ quarter] += product(halves(residue), other, 1, 0)


def setup_kernel(latent_ref, left_ref, right_ref, kind_ref, edges_ref, rows_ref, ids_ref, coded_ref, kinds_ref, ints_ref, sems):
    copies = [
        pltpu.make_async_copy(source, target, sems.at[at])
        for at, (source, target) in enumerate(
            (
                (kind_ref, kinds_ref),
                (edges_ref, ints_ref),
                (left_ref, ids_ref.at[0]),
                (right_ref, ids_ref.at[1]),
                (latent_ref, rows_ref),
            )
        )
    ]
    for copy in copies:
        copy.start()
    for copy in copies[:2]:
        copy.wait()
    peers, slots = edges_ref.shape[:2]
    for peer in range(peers):
        for slot in range(slots):
            edges = ints_ref[peer, slot].astype(F32)
            kind = jnp.broadcast_to(kinds_ref[slot : slot + 1, peer : peer + 1], edges.shape)
            coded_ref[peer, slot] = jnp.where(kind == 2, edges, -1.0)
    for copy in copies[2:]:
        copy.wait()


def add_own(total_ref, ids_ref, latent_ref, coded_ref):
    me = lax.axis_index("rows")
    quarter = lax.axis_index("pairs") * (total_ref.shape[0] // lax.axis_size("pairs"))
    for slot in range(coded_ref.shape[1]):
        left_block, right_block = ids_ref[0, slot, me], ids_ref[1, slot, me]
        left, right = halves(latent_ref[left_block]), halves(latent_ref[right_block])
        target = natural_target(coded_ref[me, slot])
        residue = halves(jax.nn.sigmoid(product(right, left, 1, 1)) - target)
        total_ref[left_block ^ quarter] += product(residue, right, 0, 0)
        total_ref[right_block ^ quarter] += product(residue, left, 1, 0)


def first_kernel(shifts, places, ids_ref, asked_ref, latent_ref, coded_ref, *refs):
    *message_refs, total_ref = refs
    total_ref[...] = jnp.zeros_like(total_ref)
    add_own(total_ref, ids_ref, latent_ref, coded_ref)
    for shift, place, message_ref in zip(shifts, places, message_refs):
        add_peer(shift, place, total_ref, ids_ref, asked_ref, latent_ref, coded_ref, message_ref)


def middle_kernel(shifts, places, ids_ref, asked_ref, latent_ref, coded_ref, before_ref, *refs):
    *message_refs, total_ref = refs
    total_ref[...] = before_ref[...]
    for shift, place, message_ref in zip(shifts, places, message_refs):
        add_peer(shift, place, total_ref, ids_ref, asked_ref, latent_ref, coded_ref, message_ref)


def last_kernel(shifts, places, ids_ref, asked_ref, latent_ref, coded_ref, before_ref, *refs):
    count = len(shifts)
    message_refs, part_refs, total_ref = refs[:count], refs[count:-1], refs[-1]
    total_ref[...] = before_ref[...]
    for shift, place, message_ref in zip(shifts, places, message_refs):
        add_peer(shift, place, total_ref, ids_ref, asked_ref, latent_ref, coded_ref, message_ref)
    for place, part_ref in enumerate(part_refs):
        depth = part_ref.shape[0]
        part_ref[...] = total_ref[place * depth : (place + 1) * depth]


def shift_groups(order, top):
    near, far = [at for at in order if at < top], [at for at in order if at >= top]
    near, far, first, last = near[1:], far[1:-2], near[:1] + far[:1], far[-2:]
    middle = [part[at : at + 2] for part in (near, far) for at in range(0, len(part), 2)]
    return [first] + middle + [last]


def estimate(slots, width, moved):
    return pl.CostEstimate(flops=12 * slots * width**3, bytes_accessed=moved, transcendentals=slots * width**2)


def swap(value, axis, shift):
    return lax.ppermute(value, axis, [(at, at ^ shift) for at in range(lax.axis_size(axis))])


def body(latent, left_block, right_block, slot_kind, edge_cols):
    tile, width = edge_cols.shape[-1], latent.shape[1]
    blocks = latent.reshape(-1, tile, width)
    peers, slots = left_block.shape[2:]
    lists = edge_cols.shape[4]

    def table(value):
        return value.reshape(peers, slots).T

    edges = edge_cols.reshape(peers, slots, lists, tile)
    blocks, ids, coded = pl.pallas_call(
        setup_kernel,
        out_shape=(
            jax.ShapeDtypeStruct(blocks.shape, F32),
            jax.ShapeDtypeStruct((2, slots, peers), jnp.int32),
            jax.ShapeDtypeStruct(edges.shape, F32),
        ),
        in_specs=[HBM] * 5,
        out_specs=(VMEM,) * 3,
        scratch_shapes=[
            pltpu.VMEM((slots, peers), jnp.int32),
            pltpu.VMEM(edges.shape, jnp.int32),
            pltpu.SemaphoreType.DMA((5,)),
        ],
        compiler_params=PARAMS,
    )(blocks, table(left_block), table(right_block), table(slot_kind), edges)

    message = jax.ShapeDtypeStruct((slots, tile + lists, width), F32)
    asked, where, arrived = right_block, [0], {}
    bit = peers // 2
    while bit:
        if len(where) == 1:
            asked = jnp.concatenate([ids[1:], table(swap(asked, "rows", bit))[None]])
        else:
            asked = jnp.concatenate([asked, swap(asked, "rows", bit)])
        where = where + [at ^ bit for at in where]
        shifts = [at for at in reversed(range(1, peers)) if at & -at == bit]
        sent = pl.pallas_call(
            functools.partial(pack_kernel, shifts, [where.index(at) for at in shifts]),
            out_shape=[message] * len(shifts),
            in_specs=[SMEM] * 2 + [VMEM] * 2,
            out_specs=[VMEM] * len(shifts),
            compiler_params=PARAMS,
        )(ids, asked, blocks, coded)
        for shift, value in zip(shifts, sent):
            arrived[shift] = swap(value, "rows", shift)
        bit //= 2

    whole = jax.ShapeDtypeStruct(blocks.shape, F32)
    parts = lax.axis_size("pairs")
    part = jax.ShapeDtypeStruct((blocks.shape[0] // parts, tile, width), F32)
    groups = shift_groups(list(arrived), peers // 2)
    total = ()
    for group in groups:
        first, last = group is groups[0], group is groups[-1]
        total = pl.pallas_call(
            functools.partial(
                first_kernel if first else last_kernel if last else middle_kernel,
                group,
                [where.index(at) for at in group],
            ),
            out_shape=[part] * parts if last else [whole],
            in_specs=[SMEM] * 2 + [VMEM] * (2 + len(total) + len(group)),
            out_specs=[VMEM] * (parts if last else 1),
            scratch_shapes=[pltpu.VMEM(blocks.shape, F32)] if last else [],
            input_output_aliases={} if first or last else {4: 0},
            compiler_params=PARAMS,
            cost_estimate=estimate(slots * len(group), tile, 3 * blocks.size * 4),
        )(ids, asked, blocks, coded, *total, *[arrived[at] for at in group])
    held = total
    far_half = held[2] + swap(held[3], "pairs", 1)
    kept = swap(held[1], "pairs", 1)
    result = held[0] + kept + swap(far_half, "pairs", 2)
    return result.reshape(-1, width)


def solution(mesh):
    return jax.shard_map(
        body,
        mesh=mesh,
        in_specs=(
            P("rows", None),
            P("rows", "pairs", None, None),
            P("rows", "pairs", None, None),
            P("rows", "pairs", None, None),
            P("rows", "pairs", None, None, None, None),
        ),
        out_specs=P(("rows", "pairs"), None),
        check_vma=False,
    )
```

```python
import functools

import jax
import jax.numpy as jnp
from jax import lax
from jax.experimental import pallas as pl
from jax.experimental.pallas import tpu as pltpu
from jax.sharding import PartitionSpec as P

F32 = jnp.float32
BF16 = jnp.bfloat16
SMEM = pl.BlockSpec(memory_space=pltpu.SMEM)
VMEM = pl.BlockSpec(memory_space=pltpu.VMEM)
HBM = pl.BlockSpec(memory_space=pltpu.HBM)
WAIT_FLOPS = 10**10
PARAMS = pltpu.CompilerParams(vmem_limit_bytes=16 * 1024 * 1024)


def halves(value):
    high = value.astype(BF16)
    return high, (value - high.astype(F32)).astype(BF16)


def product(left, right, left_dim, right_dim):
    deep = jnp.concatenate(left, left_dim)
    both = [jnp.concatenate([half, half], right_dim) for half in right]
    wide = jnp.concatenate(both, 1 - right_dim)
    sums = lax.dot_general(
        deep, wide, (((left_dim,), (right_dim,)), ((), ())), preferred_element_type=F32
    )
    width = sums.shape[1] // 2
    return sums[:, :width] + sums[:, width:]


def natural_target(edges):
    width = edges.shape[-1]
    row = lax.broadcasted_iota(jnp.int32, (width, width), 0).astype(F32)
    hit = row == edges[0:1, :]
    for which in range(1, edges.shape[0]):
        hit = hit | (row == edges[which : which + 1, :])
    return jnp.where(hit, 1.0, 0.0)


def own_id(ids_ref, asked_ref, place, me, peer, slot):
    return jnp.where(peer > me, ids_ref[0, slot, peer], asked_ref[place, slot, me])


def pack_kernel(shifts, places, ids_ref, asked_ref, latent_ref, coded_ref, *message_refs):
    me = lax.axis_index("rows")
    tile = latent_ref.shape[1]
    for shift, place, message_ref in zip(shifts, places, message_refs):
        peer = me ^ shift
        for slot in range(message_ref.shape[0]):
            block = own_id(ids_ref, asked_ref, place, me, peer, slot)
            message_ref[slot, :tile] = latent_ref[block]
            message_ref[slot, tile:] = coded_ref[peer, slot]


def add_peer(shift, place, total_ref, ids_ref, asked_ref, latent_ref, coded_ref, message_ref):
    me = lax.axis_index("rows")
    peer = me ^ shift
    low = peer > me
    quarter = lax.axis_index("pairs") * (total_ref.shape[0] // lax.axis_size("pairs"))
    tile = latent_ref.shape[1]
    for slot in range(message_ref.shape[0]):
        block = own_id(ids_ref, asked_ref, place, me, peer, slot)
        own = halves(latent_ref[block])
        other = halves(message_ref[slot, :tile])
        edges = jnp.where(low, coded_ref[peer, slot], message_ref[slot, tile:])
        target = natural_target(edges)
        target = jnp.where(low, target.T, target)
        residue = jax.nn.sigmoid(product(own, other, 1, 1)) - target
        total_ref[block ^ quarter] += product(halves(residue), other, 1, 0)


def copy_kernel(source_ref, target_ref):
    target_ref[...] = source_ref[...]


def setup_kernel(latent_ref, left_ref, right_ref, kind_ref, edges_ref, rows_ref, ids_ref, coded_ref, kinds_ref, ints_ref, sems):
    copies = [
        pltpu.make_async_copy(source, target, sems.at[at])
        for at, (source, target) in enumerate(
            (
                (kind_ref, kinds_ref),
                (edges_ref, ints_ref),
                (left_ref, ids_ref.at[0]),
                (right_ref, ids_ref.at[1]),
                (latent_ref, rows_ref),
            )
        )
    ]
    for copy in copies:
        copy.start()
    for copy in copies[:2]:
        copy.wait()
    peers, slots = edges_ref.shape[:2]
    for peer in range(peers):
        for slot in range(slots):
            edges = ints_ref[peer, slot].astype(F32)
            kind = jnp.broadcast_to(kinds_ref[slot : slot + 1, peer : peer + 1], edges.shape)
            coded_ref[peer, slot] = jnp.where(kind == 2, edges, -1.0)
    for copy in copies[2:]:
        copy.wait()


def add_own(total_ref, ids_ref, latent_ref, coded_ref):
    me = lax.axis_index("rows")
    quarter = lax.axis_index("pairs") * (total_ref.shape[0] // lax.axis_size("pairs"))
    for slot in range(coded_ref.shape[1]):
        left_block, right_block = ids_ref[0, slot, me], ids_ref[1, slot, me]
        left, right = halves(latent_ref[left_block]), halves(latent_ref[right_block])
        target = natural_target(coded_ref[me, slot])
        residue = halves(jax.nn.sigmoid(product(right, left, 1, 1)) - target)
        total_ref[left_block ^ quarter] += product(residue, right, 0, 0)
        total_ref[right_block ^ quarter] += product(residue, left, 1, 0)


def first_kernel(shifts, places, ids_ref, asked_ref, latent_ref, coded_ref, *refs):
    *message_refs, total_ref = refs
    total_ref[...] = jnp.zeros_like(total_ref)
    add_own(total_ref, ids_ref, latent_ref, coded_ref)
    for shift, place, message_ref in zip(shifts, places, message_refs):
        add_peer(shift, place, total_ref, ids_ref, asked_ref, latent_ref, coded_ref, message_ref)


def middle_kernel(shifts, places, ids_ref, asked_ref, latent_ref, coded_ref, before_ref, *refs):
    *message_refs, total_ref = refs
    total_ref[...] = before_ref[...]
    for shift, place, message_ref in zip(shifts, places, message_refs):
        add_peer(shift, place, total_ref, ids_ref, asked_ref, latent_ref, coded_ref, message_ref)


def last_kernel(shifts, places, ids_ref, asked_ref, latent_ref, coded_ref, before_ref, *refs):
    count = len(shifts)
    message_refs, part_refs, total_ref = refs[:count], refs[count:-1], refs[-1]
    total_ref[...] = before_ref[...]
    for shift, place, message_ref in zip(shifts, places, message_refs):
        add_peer(shift, place, total_ref, ids_ref, asked_ref, latent_ref, coded_ref, message_ref)
    for place, part_ref in enumerate(part_refs):
        depth = part_ref.shape[0]
        part_ref[...] = total_ref[place * depth : (place + 1) * depth]


def shift_groups(peers):
    top = peers // 2
    sequence, bit = [], top
    while bit:
        stage = [at for at in reversed(range(1, peers)) if at & -at == bit]
        sequence += sorted(stage, key=lambda at: (at < top) != (bit == 1))
        bit //= 2
    middle = sequence[1:-2]
    return [sequence[:1]] + [middle[at : at + 2] for at in range(0, len(middle), 2)] + [[at] for at in sequence[-2:]]


def estimate(slots, width, moved):
    return pl.CostEstimate(flops=12 * slots * width**3, bytes_accessed=moved, transcendentals=slots * width**2)


def swap(value, axis, shift):
    return lax.ppermute(value, axis, [(at, at ^ shift) for at in range(lax.axis_size(axis))])


def body(latent, left_block, right_block, slot_kind, edge_cols):
    tile, width = edge_cols.shape[-1], latent.shape[1]
    blocks = latent.reshape(-1, tile, width)
    peers, slots = left_block.shape[2:]
    lists = edge_cols.shape[4]

    def table(value):
        return value.reshape(peers, slots).T

    edges = edge_cols.reshape(peers, slots, lists, tile)
    own_asked = pl.pallas_call(
        copy_kernel,
        out_shape=jax.ShapeDtypeStruct((slots, peers), jnp.int32),
        in_specs=[VMEM],
        out_specs=VMEM,
        compiler_params=PARAMS,
        cost_estimate=pl.CostEstimate(flops=WAIT_FLOPS, bytes_accessed=4096, transcendentals=0),
    )(table(right_block))
    blocks, ids, coded = pl.pallas_call(
        setup_kernel,
        out_shape=(
            jax.ShapeDtypeStruct(blocks.shape, F32),
            jax.ShapeDtypeStruct((2, slots, peers), jnp.int32),
            jax.ShapeDtypeStruct(edges.shape, F32),
        ),
        in_specs=[HBM] * 5,
        out_specs=(VMEM,) * 3,
        scratch_shapes=[
            pltpu.VMEM((slots, peers), jnp.int32),
            pltpu.VMEM(edges.shape, jnp.int32),
            pltpu.SemaphoreType.DMA((5,)),
        ],
        compiler_params=PARAMS,
    )(blocks, table(left_block), own_asked, table(slot_kind), edges)

    message = jax.ShapeDtypeStruct((slots, tile + lists, width), F32)
    asked, where, arrived = own_asked, [0], {}
    bit = peers // 2
    while bit:
        if len(where) == 1:
            asked = jnp.concatenate([ids[1:], swap(asked, "rows", bit)[None]])
        else:
            asked = jnp.concatenate([asked, swap(asked, "rows", bit)])
        where = where + [at ^ bit for at in where]
        shifts = [at for at in reversed(range(1, peers)) if at & -at == bit]
        sent = pl.pallas_call(
            functools.partial(pack_kernel, shifts, [where.index(at) for at in shifts]),
            out_shape=[message] * len(shifts),
            in_specs=[SMEM] * 2 + [VMEM] * 2,
            out_specs=[VMEM] * len(shifts),
            compiler_params=PARAMS,
        )(ids, asked, blocks, coded)
        for shift, value in zip(shifts, sent):
            arrived[shift] = swap(value, "rows", shift)
        bit //= 2

    whole = jax.ShapeDtypeStruct(blocks.shape, F32)
    parts = lax.axis_size("pairs")
    part = jax.ShapeDtypeStruct((blocks.shape[0] // parts, tile, width), F32)
    groups = shift_groups(peers)
    total = ()
    for group in groups:
        first, last = group is groups[0], group is groups[-1]
        total = pl.pallas_call(
            functools.partial(
                first_kernel if first else last_kernel if last else middle_kernel,
                group,
                [where.index(at) for at in group],
            ),
            out_shape=[part] * parts if last else [whole],
            in_specs=[SMEM] * 2 + [VMEM] * (2 + len(total) + len(group)),
            out_specs=[VMEM] * (parts if last else 1),
            scratch_shapes=[pltpu.VMEM(blocks.shape, F32)] if last else [],
            input_output_aliases={} if first or last else {4: 0},
            compiler_params=PARAMS,
            cost_estimate=estimate(slots * len(group), tile, 3 * blocks.size * 4),
        )(ids, asked, blocks, coded, *total, *[arrived[at] for at in group])
    held = total
    far_half = held[2] + swap(held[3], "pairs", 1)
    kept = swap(held[1], "pairs", 1)
    result = held[0] + kept + swap(far_half, "pairs", 2)
    return result.reshape(-1, width)


def solution(mesh):
    return jax.shard_map(
        body,
        mesh=mesh,
        in_specs=(
            P("rows", None),
            P("rows", "pairs", None, None),
            P("rows", "pairs", None, None),
            P("rows", "pairs", None, None),
            P("rows", "pairs", None, None, None, None),
        ),
        out_specs=P(("rows", "pairs"), None),
        check_vma=False,
    )
```

```python
import functools

import jax
import jax.numpy as jnp
from jax import lax
from jax.experimental import pallas as pl
from jax.experimental.pallas import tpu as pltpu
from jax.sharding import PartitionSpec as P

F32 = jnp.float32
BF16 = jnp.bfloat16
SMEM = pl.BlockSpec(memory_space=pltpu.SMEM)
VMEM = pl.BlockSpec(memory_space=pltpu.VMEM)
HBM = pl.BlockSpec(memory_space=pltpu.HBM)
WAIT_FLOPS = 10**10
PARAMS = pltpu.CompilerParams(vmem_limit_bytes=16 * 1024 * 1024)


def halves(value):
    high = value.astype(BF16)
    return high, (value - high.astype(F32)).astype(BF16)


def product(left, right, left_dim, right_dim):
    deep = jnp.concatenate(left, left_dim)
    both = [jnp.concatenate([half, half], right_dim) for half in right]
    wide = jnp.concatenate(both, 1 - right_dim)
    sums = lax.dot_general(
        deep, wide, (((left_dim,), (right_dim,)), ((), ())), preferred_element_type=F32
    )
    width = sums.shape[1] // 2
    return sums[:, :width] + sums[:, width:]


def natural_target(edges):
    width = edges.shape[-1]
    row = lax.broadcasted_iota(jnp.int32, (width, width), 0).astype(F32)
    hit = row == edges[0:1, :]
    for which in range(1, edges.shape[0]):
        hit = hit | (row == edges[which : which + 1, :])
    return jnp.where(hit, 1.0, 0.0)


def own_id(ids_ref, asked_ref, place, me, peer, slot):
    return jnp.where(peer > me, ids_ref[0, slot, peer], asked_ref[place, slot, me])


def pack_kernel(shifts, places, ids_ref, asked_ref, latent_ref, coded_ref, passed_ref, *message_refs):
    me = lax.axis_index("rows")
    tile = latent_ref.shape[1]
    top, _, lists, _ = passed_ref.shape
    for shift, place, message_ref in zip(shifts, places, message_refs):
        peer = me ^ shift
        for slot in range(message_ref.shape[0]):
            block = own_id(ids_ref, asked_ref, place, me, peer, slot)
            message_ref[slot, :tile] = latent_ref[block]
            if shift < top:
                message_ref[slot, tile : tile + lists] = coded_ref[peer, slot]
                message_ref[slot, tile + lists :] = passed_ref[lax.rem(peer, top), slot]


def sent_edges(shift, coded_ref, carrier_ref, me, slot):
    _, _, lists, tile = coded_ref.shape
    top = coded_ref.shape[0] // 2
    if shift == top:
        return carrier_ref[lax.rem(me, top), slot]
    start = tile if shift < top else tile + lists
    return carrier_ref[slot, start : start + lists]


def slot_target(shift, coded_ref, carrier_ref, slot):
    me = lax.axis_index("rows")
    peer = me ^ shift
    low = peer > me
    target = natural_target(jnp.where(low, coded_ref[peer, slot], sent_edges(shift, coded_ref, carrier_ref, me, slot)))
    return jnp.where(low, target.T, target)


def add_peer(shift, place, total_ref, ids_ref, asked_ref, latent_ref, coded_ref, message_ref, carrier_ref):
    me = lax.axis_index("rows")
    peer = me ^ shift
    quarter = lax.axis_index("pairs") * (total_ref.shape[0] // lax.axis_size("pairs"))
    tile = latent_ref.shape[1]
    for slot in range(message_ref.shape[0]):
        block = own_id(ids_ref, asked_ref, place, me, peer, slot)
        own = halves(latent_ref[block])
        other = halves(message_ref[slot, :tile])
        target = slot_target(shift, coded_ref, carrier_ref, slot)
        residue = jax.nn.sigmoid(product(own, other, 1, 1)) - target
        total_ref[block ^ quarter] += product(halves(residue), other, 1, 0)


def tables_kernel(left_ref, right_ref, kind_ref, asked_ref, ids_ref, kinds_ref):
    asked_ref[...] = right_ref[...]
    ids_ref[0] = left_ref[...]
    ids_ref[1] = right_ref[...]
    kinds_ref[...] = kind_ref[...]


def setup_kernel(kinds_ref, latent_ref, edges_ref, rows_ref, coded_ref, far_ref, ints_ref, sems):
    copies = [
        pltpu.make_async_copy(source, target, sems.at[at])
        for at, (source, target) in enumerate(((edges_ref, ints_ref), (latent_ref, rows_ref)))
    ]
    for copy in copies:
        copy.start()
    copies[0].wait()
    peers, slots = edges_ref.shape[:2]
    for peer in range(peers):
        for slot in range(slots):
            edges = ints_ref[peer, slot].astype(F32)
            kind = jnp.broadcast_to(kinds_ref[slot : slot + 1, peer : peer + 1], edges.shape)
            coded_ref[peer, slot] = jnp.where(kind == 2, edges, -1.0)
    far_ref[...] = coded_ref[far_ref.shape[0] :]
    copies[1].wait()


def add_own(total_ref, ids_ref, latent_ref, coded_ref):
    me = lax.axis_index("rows")
    quarter = lax.axis_index("pairs") * (total_ref.shape[0] // lax.axis_size("pairs"))
    for slot in range(coded_ref.shape[1]):
        left_block, right_block = ids_ref[0, slot, me], ids_ref[1, slot, me]
        left, right = halves(latent_ref[left_block]), halves(latent_ref[right_block])
        target = natural_target(coded_ref[me, slot])
        residue = halves(jax.nn.sigmoid(product(right, left, 1, 1)) - target)
        total_ref[left_block ^ quarter] += product(residue, right, 0, 0)
        total_ref[right_block ^ quarter] += product(residue, left, 1, 0)


def add_peers(shifts, places, total_ref, *refs):
    fixed, refs = refs[:4], refs[4:]
    count = len(shifts)
    for shift, place, message_ref, carrier_ref in zip(shifts, places, refs[:count], refs[count:]):
        add_peer(shift, place, total_ref, *fixed, message_ref, carrier_ref)


def first_kernel(shifts, places, *refs):
    *refs, total_ref = refs
    ids_ref, _, latent_ref, coded_ref = refs[:4]
    total_ref[...] = jnp.zeros_like(total_ref)
    add_own(total_ref, ids_ref, latent_ref, coded_ref)
    add_peers(shifts, places, total_ref, *refs)


def middle_kernel(shifts, places, before_ref, *refs):
    *refs, total_ref = refs
    total_ref[...] = before_ref[...]
    add_peers(shifts, places, total_ref, *refs)


def last_kernel(shifts, places, before_ref, *refs):
    count = 4 + 2 * len(shifts)
    refs, part_refs, total_ref = refs[:count], refs[count:-1], refs[-1]
    total_ref[...] = before_ref[...]
    add_peers(shifts, places, total_ref, *refs)
    for place, part_ref in enumerate(part_refs):
        depth = part_ref.shape[0]
        part_ref[...] = total_ref[place * depth : (place + 1) * depth]


def shift_groups(peers):
    top = peers // 2
    sequence, bit = [], top
    while bit:
        stage = [at for at in reversed(range(1, peers)) if at & -at == bit]
        sequence += sorted(stage, key=lambda at: (at < top) != (bit == 1))
        bit //= 2
    middle = sequence[1:-2]
    return [sequence[:1]] + [middle[at : at + 2] for at in range(0, len(middle), 2)] + [[at] for at in sequence[-2:]]


def estimate(slots, width, moved):
    return pl.CostEstimate(flops=12 * slots * width**3, bytes_accessed=moved, transcendentals=slots * width**2)


def swap(value, axis, shift):
    return lax.ppermute(value, axis, [(at, at ^ shift) for at in range(lax.axis_size(axis))])


def body(latent, left_block, right_block, slot_kind, edge_cols):
    tile, width = edge_cols.shape[-1], latent.shape[1]
    blocks = latent.reshape(-1, tile, width)
    peers, slots = left_block.shape[2:]
    lists = edge_cols.shape[4]

    def table(value):
        return value.reshape(peers, slots).T

    edges = edge_cols.reshape(peers, slots, lists, tile)
    top = peers // 2
    small = jax.ShapeDtypeStruct((slots, peers), jnp.int32)
    own_asked, ids, kinds = pl.pallas_call(
        tables_kernel,
        out_shape=(small, jax.ShapeDtypeStruct((2, slots, peers), jnp.int32), small),
        in_specs=[VMEM] * 3,
        out_specs=(VMEM,) * 3,
        compiler_params=PARAMS,
        cost_estimate=pl.CostEstimate(flops=WAIT_FLOPS, bytes_accessed=4096, transcendentals=0),
    )(table(left_block), table(right_block), table(slot_kind))
    blocks, coded, far_coded = pl.pallas_call(
        setup_kernel,
        out_shape=(
            jax.ShapeDtypeStruct(blocks.shape, F32),
            jax.ShapeDtypeStruct(edges.shape, F32),
            jax.ShapeDtypeStruct((top, *edges.shape[1:]), F32),
        ),
        in_specs=[VMEM] + [HBM] * 2,
        out_specs=(VMEM,) * 3,
        scratch_shapes=[
            pltpu.VMEM(edges.shape, jnp.int32),
            pltpu.SemaphoreType.DMA((2,)),
        ],
        compiler_params=PARAMS,
    )(kinds, blocks, edges)

    passed = swap(far_coded, "rows", top)
    near_message = jax.ShapeDtypeStruct((slots, tile + 2 * lists, width), F32)
    far_message = jax.ShapeDtypeStruct((slots, tile, width), F32)
    asked, where, arrived = own_asked, [0], {}
    bit = top
    while bit:
        if len(where) == 1:
            asked = jnp.concatenate([ids[1:], swap(asked, "rows", bit)[None]])
        else:
            asked = jnp.concatenate([asked, swap(asked, "rows", bit)])
        where = where + [at ^ bit for at in where]
        shifts = [at for at in reversed(range(1, peers)) if at & -at == bit]
        sent = pl.pallas_call(
            functools.partial(pack_kernel, shifts, [where.index(at) for at in shifts]),
            out_shape=[far_message if at >= top else near_message for at in shifts],
            in_specs=[SMEM] * 2 + [VMEM] * 3,
            out_specs=[VMEM] * len(shifts),
            compiler_params=PARAMS,
        )(ids, asked, blocks, coded, passed if bit < top else coded[:top])
        for shift, value in zip(shifts, sent):
            arrived[shift] = swap(value, "rows", shift)
        bit //= 2

    whole = jax.ShapeDtypeStruct(blocks.shape, F32)
    parts = lax.axis_size("pairs")
    part = jax.ShapeDtypeStruct((blocks.shape[0] // parts, tile, width), F32)
    groups = shift_groups(peers)
    carrier = {at: passed if at == top else arrived[at % top] for at in arrived}
    total = ()
    for group in groups:
        first, last = group is groups[0], group is groups[-1]
        total = pl.pallas_call(
            functools.partial(
                first_kernel if first else last_kernel if last else middle_kernel,
                group,
                [where.index(at) for at in group],
            ),
            out_shape=[part] * parts if last else [whole],
            in_specs=[VMEM] * len(total) + [SMEM] * 2 + [VMEM] * (2 + 2 * len(group)),
            out_specs=[VMEM] * (parts if last else 1),
            scratch_shapes=[pltpu.VMEM(blocks.shape, F32)] if last else [],
            input_output_aliases={} if first or last else {0: 0},
            compiler_params=PARAMS,
            cost_estimate=estimate(slots * len(group), tile, 3 * blocks.size * 4),
        )(*total, ids, asked, blocks, coded, *[arrived[at] for at in group], *[carrier[at] for at in group])
    held = total
    far_half = held[2] + swap(held[3], "pairs", 1)
    kept = swap(held[1], "pairs", 1)
    result = held[0] + kept + swap(far_half, "pairs", 2)
    return result.reshape(-1, width)


def solution(mesh):
    return jax.shard_map(
        body,
        mesh=mesh,
        in_specs=(
            P("rows", None),
            P("rows", "pairs", None, None),
            P("rows", "pairs", None, None),
            P("rows", "pairs", None, None),
            P("rows", "pairs", None, None, None, None),
        ),
        out_specs=P(("rows", "pairs"), None),
        check_vma=False,
    )
```

```python
import functools

import jax
import jax.numpy as jnp
from jax import lax
from jax.experimental import pallas as pl
from jax.experimental.pallas import tpu as pltpu
from jax.sharding import PartitionSpec as P

F32 = jnp.float32
BF16 = jnp.bfloat16
VMEM = pl.BlockSpec(memory_space=pltpu.VMEM)
HBM = pl.BlockSpec(memory_space=pltpu.HBM)
WAIT_FLOPS = 10**10
PARAMS = pltpu.CompilerParams(vmem_limit_bytes=16 * 1024 * 1024)


def halves(value):
    high = value.astype(BF16)
    return high, (value - high.astype(F32)).astype(BF16)


def product(left, right, left_dim, right_dim):
    deep = jnp.concatenate(left, left_dim)
    both = [jnp.concatenate([half, half], right_dim) for half in right]
    wide = jnp.concatenate(both, 1 - right_dim)
    sums = lax.dot_general(
        deep, wide, (((left_dim,), (right_dim,)), ((), ())), preferred_element_type=F32
    )
    width = sums.shape[1] // 2
    return sums[:, :width] + sums[:, width:]


def natural_target(edges):
    width = edges.shape[-1]
    row = lax.broadcasted_iota(jnp.int32, (width, width), 0).astype(F32)
    hit = row == edges[0:1, :]
    for which in range(1, edges.shape[0]):
        hit = hit | (row == edges[which : which + 1, :])
    return jnp.where(hit, 1.0, 0.0)


def picked(table, column):
    columns = lax.broadcasted_iota(jnp.int32, table.shape, 1)
    hits = jnp.where(columns == column, table, 0).astype(F32)
    return [jnp.sum(hits[slot : slot + 1]).astype(jnp.int32) for slot in range(table.shape[0])]


def own_blocks(shift, place, ids_ref, asked_ref):
    me = lax.axis_index("rows")
    peer = me ^ shift
    low = peer > me
    return picked(jnp.where(low, ids_ref[0], asked_ref[place]), jnp.where(low, peer, me))


def pack_kernel(shifts, places, ids_ref, asked_ref, latent_ref, coded_ref, passed_ref, *message_refs):
    me = lax.axis_index("rows")
    tile = latent_ref.shape[1]
    top, _, lists, _ = passed_ref.shape
    for shift, place, message_ref in zip(shifts, places, message_refs):
        peer = me ^ shift
        for slot, block in enumerate(own_blocks(shift, place, ids_ref, asked_ref)):
            message_ref[slot, :tile] = latent_ref[block]
            if shift < top:
                message_ref[slot, tile : tile + lists] = coded_ref[peer, slot]
                message_ref[slot, tile + lists :] = passed_ref[lax.rem(peer, top), slot]


def sent_edges(shift, coded_ref, carrier_ref, me, slot):
    _, _, lists, tile = coded_ref.shape
    top = coded_ref.shape[0] // 2
    if shift == top:
        return carrier_ref[lax.rem(me, top), slot]
    start = tile if shift < top else tile + lists
    return carrier_ref[slot, start : start + lists]


def slot_target(shift, coded_ref, carrier_ref, slot):
    me = lax.axis_index("rows")
    peer = me ^ shift
    low = peer > me
    target = natural_target(jnp.where(low, coded_ref[peer, slot], sent_edges(shift, coded_ref, carrier_ref, me, slot)))
    return jnp.where(low, target.T, target)


def add_peer(shift, place, total_ref, ids_ref, asked_ref, coded_ref, sent_ref, message_ref, carrier_ref):
    quarter = lax.axis_index("pairs") * (total_ref.shape[0] // lax.axis_size("pairs"))
    tile = coded_ref.shape[-1]
    for slot, block in enumerate(own_blocks(shift, place, ids_ref, asked_ref)):
        own = halves(sent_ref[slot, :tile])
        other = halves(message_ref[slot, :tile])
        target = slot_target(shift, coded_ref, carrier_ref, slot)
        residue = jax.nn.sigmoid(product(own, other, 1, 1)) - target
        total_ref[block ^ quarter] += product(halves(residue), other, 1, 0)


def tables_kernel(left_ref, right_ref, kind_ref, asked_ref, ids_ref, kinds_ref):
    asked_ref[...] = right_ref[...]
    ids_ref[0] = left_ref[...]
    ids_ref[1] = right_ref[...]
    kinds_ref[...] = kind_ref[...]


def setup_kernel(kinds_ref, latent_ref, edges_ref, rows_ref, coded_ref, far_ref, ints_ref, sems):
    copies = [
        pltpu.make_async_copy(source, target, sems.at[at])
        for at, (source, target) in enumerate(((edges_ref, ints_ref), (latent_ref, rows_ref)))
    ]
    for copy in copies:
        copy.start()
    copies[0].wait()
    peers, slots = edges_ref.shape[:2]
    for peer in range(peers):
        for slot in range(slots):
            edges = ints_ref[peer, slot].astype(F32)
            kind = jnp.broadcast_to(kinds_ref[slot : slot + 1, peer : peer + 1], edges.shape)
            coded_ref[peer, slot] = jnp.where(kind == 2, edges, -1.0)
    far_ref[...] = coded_ref[far_ref.shape[0] :]
    copies[1].wait()


def add_own(total_ref, ids_ref, latent_ref, coded_ref):
    me = lax.axis_index("rows")
    quarter = lax.axis_index("pairs") * (total_ref.shape[0] // lax.axis_size("pairs"))
    ids = zip(picked(ids_ref[0], me), picked(ids_ref[1], me))
    for slot, (left_block, right_block) in enumerate(ids):
        left, right = halves(latent_ref[left_block]), halves(latent_ref[right_block])
        target = natural_target(coded_ref[me, slot])
        residue = halves(jax.nn.sigmoid(product(right, left, 1, 1)) - target)
        total_ref[left_block ^ quarter] += product(residue, right, 0, 0)
        total_ref[right_block ^ quarter] += product(residue, left, 1, 0)


def add_peers(shifts, places, total_ref, *refs):
    fixed, refs = refs[:3], refs[3:]
    for at, (shift, place) in enumerate(zip(shifts, places)):
        add_peer(shift, place, total_ref, *fixed, *refs[3 * at : 3 * at + 3])


def first_kernel(shifts, places, latent_ref, *refs):
    *refs, total_ref = refs
    ids_ref, _, coded_ref = refs[:3]
    total_ref[...] = jnp.zeros_like(total_ref)
    add_own(total_ref, ids_ref, latent_ref, coded_ref)
    add_peers(shifts, places, total_ref, *refs)


def middle_kernel(shifts, places, before_ref, *refs):
    *refs, total_ref = refs
    total_ref[...] = before_ref[...]
    add_peers(shifts, places, total_ref, *refs)


def last_kernel(shifts, places, before_ref, *refs):
    count = 3 + 3 * len(shifts)
    refs, part_refs, total_ref = refs[:count], refs[count:-1], refs[-1]
    total_ref[...] = before_ref[...]
    add_peers(shifts, places, total_ref, *refs)
    for place, part_ref in enumerate(part_refs):
        depth = part_ref.shape[0]
        part_ref[...] = total_ref[place * depth : (place + 1) * depth]


def shift_groups(peers):
    top = peers // 2
    sequence, bit = [], top
    while bit:
        stage = [at for at in reversed(range(1, peers)) if at & -at == bit]
        sequence += sorted(stage, key=lambda at: (at < top) != (bit == 1))
        bit //= 2
    middle = sequence[1:-2]
    return [sequence[:1]] + [middle[at : at + 2] for at in range(0, len(middle), 2)] + [[at] for at in sequence[-2:]]


def estimate(slots, width, moved):
    return pl.CostEstimate(flops=12 * slots * width**3, bytes_accessed=moved, transcendentals=slots * width**2)


def swap(value, axis, shift):
    return lax.ppermute(value, axis, [(at, at ^ shift) for at in range(lax.axis_size(axis))])


def body(latent, left_block, right_block, slot_kind, edge_cols):
    tile, width = edge_cols.shape[-1], latent.shape[1]
    blocks = latent.reshape(-1, tile, width)
    peers, slots = left_block.shape[2:]
    lists = edge_cols.shape[4]

    def table(value):
        return value.reshape(peers, slots).T

    edges = edge_cols.reshape(peers, slots, lists, tile)
    top = peers // 2
    small = jax.ShapeDtypeStruct((slots, peers), jnp.int32)
    own_asked, ids, kinds = pl.pallas_call(
        tables_kernel,
        out_shape=(small, jax.ShapeDtypeStruct((2, slots, peers), jnp.int32), small),
        in_specs=[VMEM] * 3,
        out_specs=(VMEM,) * 3,
        compiler_params=PARAMS,
        cost_estimate=pl.CostEstimate(flops=WAIT_FLOPS, bytes_accessed=4096, transcendentals=0),
    )(table(left_block), table(right_block), table(slot_kind))
    blocks, coded, far_coded = pl.pallas_call(
        setup_kernel,
        out_shape=(
            jax.ShapeDtypeStruct(blocks.shape, F32),
            jax.ShapeDtypeStruct(edges.shape, F32),
            jax.ShapeDtypeStruct((top, *edges.shape[1:]), F32),
        ),
        in_specs=[VMEM] + [HBM] * 2,
        out_specs=(VMEM,) * 3,
        scratch_shapes=[
            pltpu.VMEM(edges.shape, jnp.int32),
            pltpu.SemaphoreType.DMA((2,)),
        ],
        compiler_params=PARAMS,
    )(kinds, blocks, edges)

    passed = swap(far_coded, "rows", top)
    near_message = jax.ShapeDtypeStruct((slots, tile + 2 * lists, width), F32)
    far_message = jax.ShapeDtypeStruct((slots, tile, width), F32)
    asked, where, leaving, arrived = own_asked, [0], {}, {}
    bit = top
    while bit:
        if len(where) == 1:
            asked = jnp.concatenate([ids[1:], swap(asked, "rows", bit)[None]])
        else:
            asked = jnp.concatenate([asked, swap(asked, "rows", bit)])
        where = where + [at ^ bit for at in where]
        shifts = [at for at in reversed(range(1, peers)) if at & -at == bit]
        sent = pl.pallas_call(
            functools.partial(pack_kernel, shifts, [where.index(at) for at in shifts]),
            out_shape=[far_message if at >= top else near_message for at in shifts],
            in_specs=[VMEM] * 5,
            out_specs=[VMEM] * len(shifts),
            compiler_params=PARAMS,
        )(ids, asked, blocks, coded, passed if bit < top else coded[:top])
        for shift, value in zip(shifts, sent):
            leaving[shift], arrived[shift] = value, swap(value, "rows", shift)
        bit //= 2

    whole = jax.ShapeDtypeStruct(blocks.shape, F32)
    parts = lax.axis_size("pairs")
    part = jax.ShapeDtypeStruct((blocks.shape[0] // parts, tile, width), F32)
    groups = shift_groups(peers)
    carrier = {at: passed if at == top else arrived[at % top] for at in arrived}
    total = [blocks]
    for group in groups:
        first, last = group is groups[0], group is groups[-1]
        messages = [value for at in group for value in (leaving[at], arrived[at], carrier[at])]
        total = pl.pallas_call(
            functools.partial(
                first_kernel if first else last_kernel if last else middle_kernel,
                group,
                [where.index(at) for at in group],
            ),
            out_shape=[part] * parts if last else [whole],
            in_specs=[VMEM] * (4 + len(messages)),
            out_specs=[VMEM] * (parts if last else 1),
            scratch_shapes=[pltpu.VMEM(blocks.shape, F32)] if last else [],
            input_output_aliases={} if first or last else {0: 0},
            compiler_params=PARAMS,
            cost_estimate=estimate(slots * len(group), tile, 3 * blocks.size * 4),
        )(*total, ids, asked, coded, *messages)
    held = total
    far_half = held[2] + swap(held[3], "pairs", 1)
    kept = swap(held[1], "pairs", 1)
    result = held[0] + kept + swap(far_half, "pairs", 2)
    return result.reshape(-1, width)


def solution(mesh):
    return jax.shard_map(
        body,
        mesh=mesh,
        in_specs=(
            P("rows", None),
            P("rows", "pairs", None, None),
            P("rows", "pairs", None, None),
            P("rows", "pairs", None, None),
            P("rows", "pairs", None, None, None, None),
        ),
        out_specs=P(("rows", "pairs"), None),
        check_vma=False,
    )
```

```python
import functools

import jax
import jax.numpy as jnp
from jax import lax
from jax.experimental import pallas as pl
from jax.experimental.pallas import tpu as pltpu
from jax.sharding import PartitionSpec as P

F32 = jnp.float32
BF16 = jnp.bfloat16
VMEM = pl.BlockSpec(memory_space=pltpu.VMEM)
HBM = pl.BlockSpec(memory_space=pltpu.HBM)
WAIT_FLOPS = 10**10
PARAMS = pltpu.CompilerParams(vmem_limit_bytes=16 * 1024 * 1024)


def halves(value):
    high = value.astype(BF16)
    return high, (value - high.astype(F32)).astype(BF16)


def product(left, right, left_dim, right_dim):
    deep = jnp.concatenate(left, left_dim)
    both = [jnp.concatenate([half, half], right_dim) for half in right]
    wide = jnp.concatenate(both, 1 - right_dim)
    sums = lax.dot_general(
        deep, wide, (((left_dim,), (right_dim,)), ((), ())), preferred_element_type=F32
    )
    width = sums.shape[1] // 2
    return sums[:, :width] + sums[:, width:]


def natural_target(edges):
    width = edges.shape[-1]
    row = lax.broadcasted_iota(jnp.int32, (width, width), 0).astype(F32)
    hit = row == edges[0:1, :]
    for which in range(1, edges.shape[0]):
        hit = hit | (row == edges[which : which + 1, :])
    return jnp.where(hit, 1.0, 0.0)


def picked(table, column):
    columns = lax.broadcasted_iota(jnp.int32, table.shape, 1)
    hits = jnp.where(columns == column, table, 0).astype(F32)
    return [jnp.sum(hits[slot : slot + 1]).astype(jnp.int32) for slot in range(table.shape[0])]


def own_blocks(shift, place, ids_ref, asked_ref):
    me = lax.axis_index("rows")
    peer = me ^ shift
    low = peer > me
    return picked(jnp.where(low, ids_ref[0], asked_ref[place]), jnp.where(low, peer, me))


def pack_kernel(shifts, places, ids_ref, asked_ref, latent_ref, coded_ref, passed_ref, *message_refs):
    me = lax.axis_index("rows")
    tile = latent_ref.shape[1]
    top, _, lists, _ = passed_ref.shape
    for shift, place, message_ref in zip(shifts, places, message_refs):
        peer = me ^ shift
        for slot, block in enumerate(own_blocks(shift, place, ids_ref, asked_ref)):
            message_ref[slot, :tile] = latent_ref[block]
            if shift < top:
                message_ref[slot, tile : tile + lists] = coded_ref[peer, slot]
                message_ref[slot, tile + lists :] = passed_ref[lax.rem(peer, top), slot]


def sent_edges(shift, coded_ref, carrier_ref, me, slot):
    _, _, lists, tile = coded_ref.shape
    top = coded_ref.shape[0] // 2
    if shift == top:
        return carrier_ref[lax.rem(me, top), slot]
    start = tile if shift < top else tile + lists
    return carrier_ref[slot, start : start + lists]


def slot_target(shift, coded_ref, carrier_ref, slot):
    me = lax.axis_index("rows")
    peer = me ^ shift
    low = peer > me
    target = natural_target(jnp.where(low, coded_ref[peer, slot], sent_edges(shift, coded_ref, carrier_ref, me, slot)))
    return jnp.where(low, target.T, target)


def peer_tiles(shift, place, ids_ref, asked_ref, coded_ref, sent_ref, message_ref, carrier_ref):
    width = coded_ref.shape[-1]
    tiles = []
    for slot, block in enumerate(own_blocks(shift, place, ids_ref, asked_ref)):
        own = halves(sent_ref[slot, :width])
        other = halves(message_ref[slot, :width])
        target = slot_target(shift, coded_ref, carrier_ref, slot)
        residue = jax.nn.sigmoid(product(own, other, 1, 1)) - target
        tiles.append((block, product(halves(residue), other, 1, 0)))
    return tiles


def wait_kernel(target_ref):
    target_ref[...] = jnp.zeros_like(target_ref)


def setup_kernel(
    waited_ref, left_ref, right_ref, kind_ref, latent_ref, edges_ref, rows_ref, ids_ref, coded_ref, far_ref, ints_ref, sems
):
    copies = [
        pltpu.make_async_copy(source, target, sems.at[at])
        for at, (source, target) in enumerate(((edges_ref, ints_ref), (latent_ref, rows_ref)))
    ]
    for copy in copies:
        copy.start()
    ids_ref[0] = left_ref[...]
    ids_ref[1] = right_ref[...]
    copies[0].wait()
    peers, slots = edges_ref.shape[:2]
    for peer in range(peers):
        for slot in range(slots):
            edges = ints_ref[peer, slot].astype(F32)
            kind = jnp.broadcast_to(kind_ref[slot : slot + 1, peer : peer + 1], edges.shape)
            coded_ref[peer, slot] = jnp.where(kind == 2, edges, -1.0)
    far_ref[...] = coded_ref[far_ref.shape[0] :]
    copies[1].wait()


def add_own(total_ref, ids_ref, latent_ref, coded_ref):
    me = lax.axis_index("rows")
    quarter = lax.axis_index("pairs") * (total_ref.shape[0] // lax.axis_size("pairs"))
    ids = zip(picked(ids_ref[0], me), picked(ids_ref[1], me))
    for slot, (left_block, right_block) in enumerate(ids):
        left, right = halves(latent_ref[left_block]), halves(latent_ref[right_block])
        target = natural_target(coded_ref[me, slot])
        residue = halves(jax.nn.sigmoid(product(right, left, 1, 1)) - target)
        total_ref[left_block ^ quarter] += product(residue, right, 0, 0)
        total_ref[right_block ^ quarter] += product(residue, left, 1, 0)


def add_peers(shifts, places, total_ref, *refs):
    fixed, refs = refs[:3], refs[3:]
    quarter = lax.axis_index("pairs") * (total_ref.shape[0] // lax.axis_size("pairs"))
    for at, (shift, place) in enumerate(zip(shifts, places)):
        for block, tile in peer_tiles(shift, place, *fixed, *refs[3 * at : 3 * at + 3]):
            total_ref[block ^ quarter] += tile


def first_kernel(shifts, places, latent_ref, *refs):
    *refs, total_ref = refs
    ids_ref, _, coded_ref = refs[:3]
    total_ref[...] = jnp.zeros_like(total_ref)
    add_own(total_ref, ids_ref, latent_ref, coded_ref)
    add_peers(shifts, places, total_ref, *refs)


def middle_kernel(shifts, places, before_ref, *refs):
    *refs, total_ref = refs
    total_ref[...] = before_ref[...]
    add_peers(shifts, places, total_ref, *refs)


def last_kernel(shifts, places, before_ref, ids_ref, asked_ref, coded_ref, *refs):
    count = 3 * len(shifts)
    refs, part_refs = refs[:count], refs[count:]
    tiles = []
    for at, (shift, place) in enumerate(zip(shifts, places)):
        tiles += peer_tiles(shift, place, ids_ref, asked_ref, coded_ref, *refs[3 * at : 3 * at + 3])
    depth = part_refs[0].shape[0]
    quarter = lax.axis_index("pairs") * depth
    for place, part_ref in enumerate(part_refs):
        part_ref[...] = before_ref[place * depth : (place + 1) * depth]
        for block, tile in tiles:
            at = (block ^ quarter) - place * depth

            @pl.when((at >= 0) & (at < depth))
            def add():
                part_ref[at] += tile


def shift_groups(peers):
    top = peers // 2
    near = sorted(range(1, top), key=lambda at: (-(at & -at), -at))
    groups = [[top]] + [[top + at, at] for at in near]
    far, last = groups.pop()
    return groups + [[last], [far]]


def estimate(slots, width, moved):
    return pl.CostEstimate(flops=12 * slots * width**3, bytes_accessed=moved, transcendentals=slots * width**2)


def swap(value, axis, shift):
    return lax.ppermute(value, axis, [(at, at ^ shift) for at in range(lax.axis_size(axis))])


def body(latent, left_block, right_block, slot_kind, edge_cols):
    tile, width = edge_cols.shape[-1], latent.shape[1]
    blocks = latent.reshape(-1, tile, width)
    peers, slots = left_block.shape[2:]
    lists = edge_cols.shape[4]

    def table(value):
        return value.reshape(peers, slots).T

    edges = edge_cols.reshape(peers, slots, lists, tile)
    top = peers // 2
    waited = pl.pallas_call(
        wait_kernel,
        out_shape=jax.ShapeDtypeStruct((8, 128), F32),
        out_specs=VMEM,
        compiler_params=PARAMS,
        cost_estimate=pl.CostEstimate(flops=WAIT_FLOPS, bytes_accessed=4096, transcendentals=0),
    )()
    blocks, ids, coded, far_coded = pl.pallas_call(
        setup_kernel,
        out_shape=(
            jax.ShapeDtypeStruct(blocks.shape, F32),
            jax.ShapeDtypeStruct((2, slots, peers), jnp.int32),
            jax.ShapeDtypeStruct(edges.shape, F32),
            jax.ShapeDtypeStruct((top, *edges.shape[1:]), F32),
        ),
        in_specs=[VMEM] * 4 + [HBM] * 2,
        out_specs=(VMEM,) * 4,
        scratch_shapes=[
            pltpu.VMEM(edges.shape, jnp.int32),
            pltpu.SemaphoreType.DMA((2,)),
        ],
        compiler_params=PARAMS,
    )(waited, table(left_block), table(right_block), table(slot_kind), blocks, edges)

    passed = swap(far_coded, "rows", top)
    near_message = jax.ShapeDtypeStruct((slots, tile + 2 * lists, width), F32)
    far_message = jax.ShapeDtypeStruct((slots, tile, width), F32)
    asked, where, leaving, arrived = right_block, [0], {}, {}
    bit = top
    while bit:
        if len(where) == 1:
            asked = jnp.concatenate([ids[1:], table(swap(asked, "rows", bit))[None]])
        else:
            asked = jnp.concatenate([asked, swap(asked, "rows", bit)])
        where = where + [at ^ bit for at in where]
        shifts = [at for at in reversed(range(1, peers)) if at & -at == bit]
        sent = pl.pallas_call(
            functools.partial(pack_kernel, shifts, [where.index(at) for at in shifts]),
            out_shape=[far_message if at >= top else near_message for at in shifts],
            in_specs=[VMEM] * 5,
            out_specs=[VMEM] * len(shifts),
            compiler_params=PARAMS,
        )(ids, asked, blocks, coded, passed if bit < top else coded[:top])
        for shift, value in zip(shifts, sent):
            leaving[shift], arrived[shift] = value, swap(value, "rows", shift)
        bit //= 2

    whole = jax.ShapeDtypeStruct(blocks.shape, F32)
    parts = lax.axis_size("pairs")
    part = jax.ShapeDtypeStruct((blocks.shape[0] // parts, tile, width), F32)
    groups = shift_groups(peers)
    carrier = {at: passed if at == top else arrived[at % top] for at in arrived}
    total = [blocks]
    for group in groups:
        first, last = group is groups[0], group is groups[-1]
        messages = [value for at in group for value in (leaving[at], arrived[at], carrier[at])]
        total = pl.pallas_call(
            functools.partial(
                first_kernel if first else last_kernel if last else middle_kernel,
                group,
                [where.index(at) for at in group],
            ),
            out_shape=[part] * parts if last else [whole],
            in_specs=[VMEM] * (4 + len(messages)),
            out_specs=[VMEM] * (parts if last else 1),
            input_output_aliases={} if first or last else {0: 0},
            compiler_params=PARAMS,
            cost_estimate=estimate(slots * len(group), tile, 3 * blocks.size * 4),
        )(*total, ids, asked, coded, *messages)
    held = total
    far_half = held[2] + swap(held[3], "pairs", 1)
    kept = swap(held[1], "pairs", 1)
    result = held[0] + kept + swap(far_half, "pairs", 2)
    return result.reshape(-1, width)


def solution(mesh):
    return jax.shard_map(
        body,
        mesh=mesh,
        in_specs=(
            P("rows", None),
            P("rows", "pairs", None, None),
            P("rows", "pairs", None, None),
            P("rows", "pairs", None, None),
            P("rows", "pairs", None, None, None, None),
        ),
        out_specs=P(("rows", "pairs"), None),
        check_vma=False,
    )
```

```python
import functools

import jax
import jax.numpy as jnp
from jax import lax
from jax.experimental import pallas as pl
from jax.experimental.pallas import tpu as pltpu
from jax.sharding import PartitionSpec as P

F32 = jnp.float32
BF16 = jnp.bfloat16
VMEM = pl.BlockSpec(memory_space=pltpu.VMEM)
HBM = pl.BlockSpec(memory_space=pltpu.HBM)
WAIT_FLOPS = 10**10
PARAMS = pltpu.CompilerParams(vmem_limit_bytes=16 * 1024 * 1024)


def halves(value):
    high = value.astype(BF16)
    return high, (value - high.astype(F32)).astype(BF16)


def product(left, right, left_dim, right_dim):
    deep = jnp.concatenate(left, left_dim)
    both = [jnp.concatenate([half, half], right_dim) for half in right]
    wide = jnp.concatenate(both, 1 - right_dim)
    sums = lax.dot_general(
        deep, wide, (((left_dim,), (right_dim,)), ((), ())), preferred_element_type=F32
    )
    width = sums.shape[1] // 2
    return sums[:, :width] + sums[:, width:]


def natural_target(edges):
    width = edges.shape[-1]
    row = lax.broadcasted_iota(jnp.int32, (width, width), 0).astype(F32)
    hit = row == edges[0:1, :]
    for which in range(1, edges.shape[0]):
        hit = hit | (row == edges[which : which + 1, :])
    return jnp.where(hit, 1.0, 0.0)


def picked(table, column):
    columns = lax.broadcasted_iota(jnp.int32, table.shape, 1)
    hits = jnp.where(columns == column, table, 0).astype(F32)
    return [jnp.sum(hits[slot : slot + 1]).astype(jnp.int32) for slot in range(table.shape[0])]


def own_blocks(shift, place, ids_ref, asked_ref):
    me = lax.axis_index("rows")
    peer = me ^ shift
    low = peer > me
    return picked(jnp.where(low, ids_ref[0], asked_ref[place]), jnp.where(low, peer, me))


def pack_kernel(shifts, places, ids_ref, asked_ref, latent_ref, coded_ref, passed_ref, *message_refs):
    me = lax.axis_index("rows")
    tile = latent_ref.shape[1]
    top, _, lists, _ = passed_ref.shape
    for shift, place, message_ref in zip(shifts, places, message_refs):
        peer = me ^ shift
        for slot, block in enumerate(own_blocks(shift, place, ids_ref, asked_ref)):
            message_ref[slot, :tile] = latent_ref[block]
            if shift < top:
                message_ref[slot, tile : tile + lists] = coded_ref[peer, slot]
                message_ref[slot, tile + lists :] = passed_ref[lax.rem(peer, top), slot]


def sent_edges(shift, coded_ref, carrier_ref, me, slot):
    _, _, lists, tile = coded_ref.shape
    top = coded_ref.shape[0] // 2
    if shift == top:
        return carrier_ref[lax.rem(me, top), slot]
    start = tile if shift < top else tile + lists
    return carrier_ref[slot, start : start + lists]


def slot_target(shift, coded_ref, carrier_ref, slot):
    me = lax.axis_index("rows")
    peer = me ^ shift
    low = peer > me
    target = natural_target(jnp.where(low, coded_ref[peer, slot], sent_edges(shift, coded_ref, carrier_ref, me, slot)))
    return jnp.where(low, target.T, target)


def peer_tiles(shift, place, ids_ref, asked_ref, coded_ref, sent_ref, message_ref, carrier_ref):
    width = coded_ref.shape[-1]
    tiles = []
    for slot, block in enumerate(own_blocks(shift, place, ids_ref, asked_ref)):
        own = halves(sent_ref[slot, :width])
        other = halves(message_ref[slot, :width])
        target = slot_target(shift, coded_ref, carrier_ref, slot)
        residue = jax.nn.sigmoid(product(own, other, 1, 1)) - target
        tiles.append((block, product(halves(residue), other, 1, 0)))
    return tiles


def wait_kernel(target_ref):
    target_ref[...] = jnp.zeros_like(target_ref)


def setup_kernel(
    waited_ref, left_ref, right_ref, kind_ref, latent_ref, edges_ref, rows_ref, ids_ref, coded_ref, far_ref, ints_ref, sems
):
    copies = [
        pltpu.make_async_copy(source, target, sems.at[at])
        for at, (source, target) in enumerate(((edges_ref, ints_ref), (latent_ref, rows_ref)))
    ]
    for copy in copies:
        copy.start()
    ids_ref[0] = left_ref[...]
    ids_ref[1] = right_ref[...]
    copies[0].wait()
    peers, slots = edges_ref.shape[:2]
    for peer in range(peers):
        for slot in range(slots):
            edges = ints_ref[peer, slot].astype(F32)
            kind = jnp.broadcast_to(kind_ref[slot : slot + 1, peer : peer + 1], edges.shape)
            coded_ref[peer, slot] = jnp.where(kind == 2, edges, -1.0)
    far_ref[...] = coded_ref[far_ref.shape[0] :]
    copies[1].wait()


def add_own(total_ref, ids_ref, latent_ref, coded_ref):
    me = lax.axis_index("rows")
    quarter = lax.axis_index("pairs") * (total_ref.shape[0] // lax.axis_size("pairs"))
    ids = zip(picked(ids_ref[0], me), picked(ids_ref[1], me))
    for slot, (left_block, right_block) in enumerate(ids):
        left, right = halves(latent_ref[left_block]), halves(latent_ref[right_block])
        target = natural_target(coded_ref[me, slot])
        residue = halves(jax.nn.sigmoid(product(right, left, 1, 1)) - target)
        total_ref[left_block ^ quarter] += product(residue, right, 0, 0)
        total_ref[right_block ^ quarter] += product(residue, left, 1, 0)


def add_peers(shifts, places, total_ref, *refs):
    fixed, refs = refs[:3], refs[3:]
    quarter = lax.axis_index("pairs") * (total_ref.shape[0] // lax.axis_size("pairs"))
    for at, (shift, place) in enumerate(zip(shifts, places)):
        for block, tile in peer_tiles(shift, place, *fixed, *refs[3 * at : 3 * at + 3]):
            total_ref[block ^ quarter] += tile


def first_kernel(shifts, places, latent_ref, *refs):
    *refs, total_ref = refs
    ids_ref, _, coded_ref = refs[:3]
    total_ref[...] = jnp.zeros_like(total_ref)
    add_own(total_ref, ids_ref, latent_ref, coded_ref)
    add_peers(shifts, places, total_ref, *refs)


def middle_kernel(shifts, places, before_ref, *refs):
    *refs, total_ref = refs
    total_ref[...] = before_ref[...]
    add_peers(shifts, places, total_ref, *refs)


def last_kernel(shifts, places, before_ref, ids_ref, asked_ref, coded_ref, *refs):
    count = 3 * len(shifts)
    refs, part_refs = refs[:count], refs[count:]
    tiles = []
    for at, (shift, place) in enumerate(zip(shifts, places)):
        tiles += peer_tiles(shift, place, ids_ref, asked_ref, coded_ref, *refs[3 * at : 3 * at + 3])
    depth = part_refs[0].shape[0]
    quarter = lax.axis_index("pairs") * depth
    for place, part_ref in enumerate(part_refs):
        part_ref[...] = before_ref[place * depth : (place + 1) * depth]
        for block, tile in tiles:
            at = (block ^ quarter) - place * depth

            @pl.when((at >= 0) & (at < depth))
            def add():
                part_ref[at] += tile


def shift_groups(peers):
    top = peers // 2
    near = sorted(range(1, top), key=lambda at: (at.bit_length(), -at))
    groups = [[top]] + [[top + at, at] for at in near]
    far, last = groups.pop()
    return groups + [[last], [far]]


def estimate(slots, width, moved):
    return pl.CostEstimate(flops=12 * slots * width**3, bytes_accessed=moved, transcendentals=slots * width**2)


def swap(value, axis, shift):
    return lax.ppermute(value, axis, [(at, at ^ shift) for at in range(lax.axis_size(axis))])


def body(latent, left_block, right_block, slot_kind, edge_cols):
    tile, width = edge_cols.shape[-1], latent.shape[1]
    blocks = latent.reshape(-1, tile, width)
    peers, slots = left_block.shape[2:]
    lists = edge_cols.shape[4]

    def table(value):
        return value.reshape(peers, slots).T

    edges = edge_cols.reshape(peers, slots, lists, tile)
    top = peers // 2
    waited = pl.pallas_call(
        wait_kernel,
        out_shape=jax.ShapeDtypeStruct((8, 128), F32),
        out_specs=VMEM,
        compiler_params=PARAMS,
        cost_estimate=pl.CostEstimate(flops=WAIT_FLOPS, bytes_accessed=4096, transcendentals=0),
    )()
    blocks, ids, coded, far_coded = pl.pallas_call(
        setup_kernel,
        out_shape=(
            jax.ShapeDtypeStruct(blocks.shape, F32),
            jax.ShapeDtypeStruct((2, slots, peers), jnp.int32),
            jax.ShapeDtypeStruct(edges.shape, F32),
            jax.ShapeDtypeStruct((top, *edges.shape[1:]), F32),
        ),
        in_specs=[VMEM] * 4 + [HBM] * 2,
        out_specs=(VMEM,) * 4,
        scratch_shapes=[
            pltpu.VMEM(edges.shape, jnp.int32),
            pltpu.SemaphoreType.DMA((2,)),
        ],
        compiler_params=PARAMS,
    )(waited, table(left_block), table(right_block), table(slot_kind), blocks, edges)

    passed = swap(far_coded, "rows", top)
    near_message = jax.ShapeDtypeStruct((slots, tile + 2 * lists, width), F32)
    far_message = jax.ShapeDtypeStruct((slots, tile, width), F32)
    asked, where, leaving, arrived = right_block, [0], {}, {}
    for bit in [top] + [1 << at for at in range(top.bit_length() - 1)]:
        if len(where) == 1:
            asked = jnp.concatenate([ids[1:], table(swap(asked, "rows", bit))[None]])
        else:
            asked = jnp.concatenate([asked, swap(asked, "rows", bit)])
        where = where + [at ^ bit for at in where]
        shifts = sorted(where[len(where) // 2 :], reverse=True)
        sent = pl.pallas_call(
            functools.partial(pack_kernel, shifts, [where.index(at) for at in shifts]),
            out_shape=[far_message if at >= top else near_message for at in shifts],
            in_specs=[VMEM] * 5,
            out_specs=[VMEM] * len(shifts),
            compiler_params=PARAMS,
        )(ids, asked, blocks, coded, passed if bit < top else coded[:top])
        for shift, value in zip(shifts, sent):
            leaving[shift], arrived[shift] = value, swap(value, "rows", shift)

    whole = jax.ShapeDtypeStruct(blocks.shape, F32)
    parts = lax.axis_size("pairs")
    part = jax.ShapeDtypeStruct((blocks.shape[0] // parts, tile, width), F32)
    groups = shift_groups(peers)
    carrier = {at: passed if at == top else arrived[at % top] for at in arrived}
    total = [blocks]
    for group in groups:
        first, last = group is groups[0], group is groups[-1]
        messages = [value for at in group for value in (leaving[at], arrived[at], carrier[at])]
        total = pl.pallas_call(
            functools.partial(
                first_kernel if first else last_kernel if last else middle_kernel,
                group,
                [where.index(at) for at in group],
            ),
            out_shape=[part] * parts if last else [whole],
            in_specs=[VMEM] * (4 + len(messages)),
            out_specs=[VMEM] * (parts if last else 1),
            input_output_aliases={} if first or last else {0: 0},
            compiler_params=PARAMS,
            cost_estimate=estimate(slots * len(group), tile, 3 * blocks.size * 4),
        )(*total, ids, asked, coded, *messages)
    held = total
    far_half = held[2] + swap(held[3], "pairs", 1)
    kept = swap(held[1], "pairs", 1)
    result = held[0] + kept + swap(far_half, "pairs", 2)
    return result.reshape(-1, width)


def solution(mesh):
    return jax.shard_map(
        body,
        mesh=mesh,
        in_specs=(
            P("rows", None),
            P("rows", "pairs", None, None),
            P("rows", "pairs", None, None),
            P("rows", "pairs", None, None),
            P("rows", "pairs", None, None, None, None),
        ),
        out_specs=P(("rows", "pairs"), None),
        check_vma=False,
    )
```

```python
import functools

import jax
import jax.numpy as jnp
from jax import lax
from jax.experimental import pallas as pl
from jax.experimental.pallas import tpu as pltpu
from jax.sharding import PartitionSpec as P

F32 = jnp.float32
BF16 = jnp.bfloat16
VMEM = pl.BlockSpec(memory_space=pltpu.VMEM)
HBM = pl.BlockSpec(memory_space=pltpu.HBM)
WAIT_FLOPS = 10**10
PARAMS = pltpu.CompilerParams(vmem_limit_bytes=16 * 1024 * 1024)


def halves(value):
    high = value.astype(BF16)
    return high, (value - high.astype(F32)).astype(BF16)


def product(left, right, left_dim, right_dim):
    deep = jnp.concatenate(left, left_dim)
    both = [jnp.concatenate([half, half], right_dim) for half in right]
    wide = jnp.concatenate(both, 1 - right_dim)
    sums = lax.dot_general(
        deep, wide, (((left_dim,), (right_dim,)), ((), ())), preferred_element_type=F32
    )
    width = sums.shape[1] // 2
    return sums[:, :width] + sums[:, width:]


def natural_target(edges):
    width = edges.shape[-1]
    row = lax.broadcasted_iota(jnp.int32, (width, width), 0).astype(F32)
    hit = row == edges[0:1, :]
    for which in range(1, edges.shape[0]):
        hit = hit | (row == edges[which : which + 1, :])
    return jnp.where(hit, 1.0, 0.0)


def picked(table, column):
    columns = lax.broadcasted_iota(jnp.int32, table.shape, 1)
    hits = jnp.where(columns == column, table, 0).astype(F32)
    return [jnp.sum(hits[slot : slot + 1]).astype(jnp.int32) for slot in range(table.shape[0])]


def own_blocks(shift, place, ids_ref, asked_ref):
    me = lax.axis_index("rows")
    peer = me ^ shift
    low = peer > me
    return picked(jnp.where(low, ids_ref[0], asked_ref[place]), jnp.where(low, peer, me))


def pack_kernel(shifts, places, ids_ref, asked_ref, latent_ref, coded_ref, passed_ref, *message_refs):
    me = lax.axis_index("rows")
    tile = latent_ref.shape[1]
    top, _, lists, _ = passed_ref.shape
    for shift, place, message_ref in zip(shifts, places, message_refs):
        peer = me ^ shift
        for slot, block in enumerate(own_blocks(shift, place, ids_ref, asked_ref)):
            message_ref[slot, :tile] = latent_ref[block]
            if shift < top:
                message_ref[slot, tile : tile + lists] = coded_ref[peer, slot]
                message_ref[slot, tile + lists :] = passed_ref[lax.rem(peer, top), slot]


def sent_edges(shift, coded_ref, carrier_ref, me, slot):
    _, _, lists, tile = coded_ref.shape
    top = coded_ref.shape[0] // 2
    if shift == top:
        return carrier_ref[lax.rem(me, top), slot]
    start = tile if shift < top else tile + lists
    return carrier_ref[slot, start : start + lists]


def slot_target(shift, coded_ref, carrier_ref, slot):
    me = lax.axis_index("rows")
    peer = me ^ shift
    low = peer > me
    target = natural_target(jnp.where(low, coded_ref[peer, slot], sent_edges(shift, coded_ref, carrier_ref, me, slot)))
    return jnp.where(low, target.T, target)


def peer_tiles(shift, place, ids_ref, asked_ref, coded_ref, sent_ref, message_ref, carrier_ref):
    width = coded_ref.shape[-1]
    tiles = []
    for slot, block in enumerate(own_blocks(shift, place, ids_ref, asked_ref)):
        own = halves(sent_ref[slot, :width])
        other = halves(message_ref[slot, :width])
        target = slot_target(shift, coded_ref, carrier_ref, slot)
        residue = jax.nn.sigmoid(product(own, other, 1, 1)) - target
        tiles.append((block, product(halves(residue), other, 1, 0)))
    return tiles


def wait_kernel(target_ref):
    target_ref[...] = jnp.zeros_like(target_ref)


def setup_kernel(
    waited_ref, left_ref, right_ref, kind_ref, latent_ref, edges_ref, rows_ref, ids_ref, coded_ref, far_ref, ints_ref, sems
):
    copies = [
        pltpu.make_async_copy(source, target, sems.at[at])
        for at, (source, target) in enumerate(((edges_ref, ints_ref), (latent_ref, rows_ref)))
    ]
    for copy in copies:
        copy.start()
    ids_ref[0] = left_ref[...]
    ids_ref[1] = right_ref[...]
    copies[0].wait()
    peers, slots = edges_ref.shape[:2]
    for peer in range(peers):
        for slot in range(slots):
            edges = ints_ref[peer, slot].astype(F32)
            kind = jnp.broadcast_to(kind_ref[slot : slot + 1, peer : peer + 1], edges.shape)
            coded_ref[peer, slot] = jnp.where(kind == 2, edges, -1.0)
    far_ref[...] = coded_ref[far_ref.shape[0] :]
    copies[1].wait()


def add_own(total_ref, ids_ref, latent_ref, coded_ref):
    me = lax.axis_index("rows")
    quarter = lax.axis_index("pairs") * (total_ref.shape[0] // lax.axis_size("pairs"))
    ids = zip(picked(ids_ref[0], me), picked(ids_ref[1], me))
    for slot, (left_block, right_block) in enumerate(ids):
        left, right = halves(latent_ref[left_block]), halves(latent_ref[right_block])
        target = natural_target(coded_ref[me, slot])
        residue = halves(jax.nn.sigmoid(product(right, left, 1, 1)) - target)
        total_ref[left_block ^ quarter] += product(residue, right, 0, 0)
        total_ref[right_block ^ quarter] += product(residue, left, 1, 0)


def add_peers(shifts, places, total_ref, *refs):
    fixed, refs = refs[:3], refs[3:]
    quarter = lax.axis_index("pairs") * (total_ref.shape[0] // lax.axis_size("pairs"))
    for at, (shift, place) in enumerate(zip(shifts, places)):
        for block, tile in peer_tiles(shift, place, *fixed, *refs[3 * at : 3 * at + 3]):
            total_ref[block ^ quarter] += tile


def first_kernel(shifts, places, latent_ref, *refs):
    *refs, total_ref = refs
    ids_ref, _, coded_ref = refs[:3]
    total_ref[...] = jnp.zeros_like(total_ref)
    add_own(total_ref, ids_ref, latent_ref, coded_ref)
    add_peers(shifts, places, total_ref, *refs)


def middle_kernel(shifts, places, before_ref, *refs):
    *refs, total_ref = refs
    total_ref[...] = before_ref[...]
    add_peers(shifts, places, total_ref, *refs)


def last_kernel(shifts, places, before_ref, ids_ref, asked_ref, coded_ref, *refs):
    count = 3 * len(shifts)
    refs, part_refs = refs[:count], refs[count:]
    tiles = []
    for at, (shift, place) in enumerate(zip(shifts, places)):
        tiles += peer_tiles(shift, place, ids_ref, asked_ref, coded_ref, *refs[3 * at : 3 * at + 3])
    depth = part_refs[0].shape[0]
    quarter = lax.axis_index("pairs") * depth
    for place, part_ref in enumerate(part_refs):
        part_ref[...] = before_ref[place * depth : (place + 1) * depth]
        for block, tile in tiles:
            at = (block ^ quarter) - place * depth

            @pl.when((at >= 0) & (at < depth))
            def add():
                part_ref[at] += tile


def shift_groups(peers):
    top = peers // 2
    near = sorted(range(1, top), key=lambda at: (at.bit_length(), at))
    return [[top]] + [[top + at, at] for at in near]


def estimate(slots, width, moved):
    return pl.CostEstimate(flops=12 * slots * width**3, bytes_accessed=moved, transcendentals=slots * width**2)


def swap(value, axis, shift):
    return lax.ppermute(value, axis, [(at, at ^ shift) for at in range(lax.axis_size(axis))])


def body(latent, left_block, right_block, slot_kind, edge_cols):
    tile, width = edge_cols.shape[-1], latent.shape[1]
    blocks = latent.reshape(-1, tile, width)
    peers, slots = left_block.shape[2:]
    lists = edge_cols.shape[4]

    def table(value):
        return value.reshape(peers, slots).T

    edges = edge_cols.reshape(peers, slots, lists, tile)
    top = peers // 2
    waited = pl.pallas_call(
        wait_kernel,
        out_shape=jax.ShapeDtypeStruct((8, 128), F32),
        out_specs=VMEM,
        compiler_params=PARAMS,
        cost_estimate=pl.CostEstimate(flops=WAIT_FLOPS, bytes_accessed=4096, transcendentals=0),
    )()
    blocks, ids, coded, far_coded = pl.pallas_call(
        setup_kernel,
        out_shape=(
            jax.ShapeDtypeStruct(blocks.shape, F32),
            jax.ShapeDtypeStruct((2, slots, peers), jnp.int32),
            jax.ShapeDtypeStruct(edges.shape, F32),
            jax.ShapeDtypeStruct((top, *edges.shape[1:]), F32),
        ),
        in_specs=[VMEM] * 4 + [HBM] * 2,
        out_specs=(VMEM,) * 4,
        scratch_shapes=[
            pltpu.VMEM(edges.shape, jnp.int32),
            pltpu.SemaphoreType.DMA((2,)),
        ],
        compiler_params=PARAMS,
    )(waited, table(left_block), table(right_block), table(slot_kind), blocks, edges)

    passed = swap(far_coded, "rows", top)
    near_message = jax.ShapeDtypeStruct((slots, tile + 2 * lists, width), F32)
    far_message = jax.ShapeDtypeStruct((slots, tile, width), F32)
    asked, where, leaving, arrived = right_block, [0], {}, {}
    for bit in [top] + [1 << at for at in range(top.bit_length() - 1)]:
        if len(where) == 1:
            asked = jnp.concatenate([ids[1:], table(swap(asked, "rows", bit))[None]])
        else:
            asked = jnp.concatenate([asked, swap(asked, "rows", bit)])
        where = where + [at ^ bit for at in where]
        shifts = sorted(where[len(where) // 2 :])
        sent = pl.pallas_call(
            functools.partial(pack_kernel, shifts, [where.index(at) for at in shifts]),
            out_shape=[far_message if at >= top else near_message for at in shifts],
            in_specs=[VMEM] * 5,
            out_specs=[VMEM] * len(shifts),
            compiler_params=PARAMS,
        )(ids, asked, blocks, coded, passed if bit < top else coded[:top])
        for shift, value in zip(shifts, sent):
            leaving[shift], arrived[shift] = value, swap(value, "rows", shift)

    whole = jax.ShapeDtypeStruct(blocks.shape, F32)
    parts = lax.axis_size("pairs")
    part = jax.ShapeDtypeStruct((blocks.shape[0] // parts, tile, width), F32)
    groups = shift_groups(peers)
    carrier = {at: passed if at == top else arrived[at % top] for at in arrived}
    total = [blocks]
    for group in groups:
        first, last = group is groups[0], group is groups[-1]
        messages = [value for at in group for value in (leaving[at], arrived[at], carrier[at])]
        total = pl.pallas_call(
            functools.partial(
                first_kernel if first else last_kernel if last else middle_kernel,
                group,
                [where.index(at) for at in group],
            ),
            out_shape=[part] * parts if last else [whole],
            in_specs=[VMEM] * (4 + len(messages)),
            out_specs=[VMEM] * (parts if last else 1),
            input_output_aliases={} if first or last else {0: 0},
            compiler_params=PARAMS,
            cost_estimate=estimate(slots * len(group), tile, 3 * blocks.size * 4),
        )(*total, ids, asked, coded, *messages)
    held = total
    far_half = held[2] + swap(held[3], "pairs", 1)
    kept = swap(held[1], "pairs", 1)
    result = held[0] + kept + swap(far_half, "pairs", 2)
    return result.reshape(-1, width)


def solution(mesh):
    return jax.shard_map(
        body,
        mesh=mesh,
        in_specs=(
            P("rows", None),
            P("rows", "pairs", None, None),
            P("rows", "pairs", None, None),
            P("rows", "pairs", None, None),
            P("rows", "pairs", None, None, None, None),
        ),
        out_specs=P(("rows", "pairs"), None),
        check_vma=False,
    )
```

```python
import functools

import jax
import jax.numpy as jnp
from jax import lax
from jax.experimental import pallas as pl
from jax.experimental.pallas import tpu as pltpu
from jax.sharding import PartitionSpec as P

F32 = jnp.float32
BF16 = jnp.bfloat16
VMEM = pl.BlockSpec(memory_space=pltpu.VMEM)
HBM = pl.BlockSpec(memory_space=pltpu.HBM)
WAIT_FLOPS = 10**10
PARAMS = pltpu.CompilerParams(vmem_limit_bytes=16 * 1024 * 1024)


def halves(value):
    high = value.astype(BF16)
    return high, (value - high.astype(F32)).astype(BF16)


def product(left, right, left_dim, right_dim):
    deep = jnp.concatenate(left, left_dim)
    both = [jnp.concatenate([half, half], right_dim) for half in right]
    wide = jnp.concatenate(both, 1 - right_dim)
    sums = lax.dot_general(
        deep, wide, (((left_dim,), (right_dim,)), ((), ())), preferred_element_type=F32
    )
    width = sums.shape[1] // 2
    return sums[:, :width] + sums[:, width:]


def natural_target(edges):
    width = edges.shape[-1]
    row = lax.broadcasted_iota(jnp.int32, (width, width), 0).astype(F32)
    hit = row == edges[0:1, :]
    for which in range(1, edges.shape[0]):
        hit = hit | (row == edges[which : which + 1, :])
    return jnp.where(hit, 1.0, 0.0)


def picked(table, column):
    columns = lax.broadcasted_iota(jnp.int32, table.shape, 1)
    hits = jnp.where(columns == column, table, 0).astype(F32)
    return [jnp.sum(hits[slot : slot + 1]).astype(jnp.int32) for slot in range(table.shape[0])]


def own_blocks(shift, place, ids_ref, asked_ref):
    me = lax.axis_index("rows")
    peer = me ^ shift
    low = peer > me
    return picked(jnp.where(low, ids_ref[0], asked_ref[place]), jnp.where(low, peer, me))


def pack_kernel(shifts, places, ids_ref, asked_ref, latent_ref, coded_ref, passed_ref, *message_refs):
    me = lax.axis_index("rows")
    tile = latent_ref.shape[1]
    top, _, lists, _ = passed_ref.shape
    for shift, place, message_ref in zip(shifts, places, message_refs):
        peer = me ^ shift
        for slot, block in enumerate(own_blocks(shift, place, ids_ref, asked_ref)):
            message_ref[slot, :tile] = latent_ref[block]
            if shift < top:
                message_ref[slot, tile : tile + lists] = coded_ref[peer, slot]
                message_ref[slot, tile + lists :] = passed_ref[lax.rem(peer, top), slot]


def sent_edges(shift, coded_ref, carrier_ref, me, slot):
    _, _, lists, tile = coded_ref.shape
    top = coded_ref.shape[0] // 2
    if shift == top:
        return carrier_ref[lax.rem(me, top), slot]
    start = tile if shift < top else tile + lists
    return carrier_ref[slot, start : start + lists]


def slot_target(shift, coded_ref, carrier_ref, slot):
    me = lax.axis_index("rows")
    peer = me ^ shift
    low = peer > me
    target = natural_target(jnp.where(low, coded_ref[peer, slot], sent_edges(shift, coded_ref, carrier_ref, me, slot)))
    return jnp.where(low, target.T, target)


def peer_tiles(shift, place, ids_ref, asked_ref, coded_ref, sent_ref, message_ref, carrier_ref):
    width = coded_ref.shape[-1]
    tiles = []
    for slot, block in enumerate(own_blocks(shift, place, ids_ref, asked_ref)):
        own = halves(sent_ref[slot, :width])
        other = halves(message_ref[slot, :width])
        target = slot_target(shift, coded_ref, carrier_ref, slot)
        residue = jax.nn.sigmoid(product(own, other, 1, 1)) - target
        tiles.append((block, product(halves(residue), other, 1, 0)))
    return tiles


def wait_kernel(target_ref):
    target_ref[...] = jnp.zeros_like(target_ref)


def setup_kernel(
    waited_ref, left_ref, right_ref, kind_ref, latent_ref, edges_ref, rows_ref, ids_ref, coded_ref, far_ref, ints_ref, sems
):
    copies = [
        pltpu.make_async_copy(source, target, sems.at[at])
        for at, (source, target) in enumerate(((edges_ref, ints_ref), (latent_ref, rows_ref)))
    ]
    for copy in copies:
        copy.start()
    ids_ref[0] = left_ref[...]
    ids_ref[1] = right_ref[...]
    copies[0].wait()
    peers, slots = edges_ref.shape[:2]
    for peer in range(peers):
        for slot in range(slots):
            edges = ints_ref[peer, slot].astype(F32)
            kind = jnp.broadcast_to(kind_ref[slot : slot + 1, peer : peer + 1], edges.shape)
            coded_ref[peer, slot] = jnp.where(kind == 2, edges, -1.0)
    far_ref[...] = coded_ref[far_ref.shape[0] :]
    copies[1].wait()


def add_own(total_ref, ids_ref, latent_ref, coded_ref):
    me = lax.axis_index("rows")
    quarter = lax.axis_index("pairs") * (total_ref.shape[0] // lax.axis_size("pairs"))
    ids = zip(picked(ids_ref[0], me), picked(ids_ref[1], me))
    for slot, (left_block, right_block) in enumerate(ids):
        left, right = halves(latent_ref[left_block]), halves(latent_ref[right_block])
        target = natural_target(coded_ref[me, slot])
        residue = halves(jax.nn.sigmoid(product(right, left, 1, 1)) - target)
        total_ref[left_block ^ quarter] += product(residue, right, 0, 0)
        total_ref[right_block ^ quarter] += product(residue, left, 1, 0)


def add_peers(shifts, places, total_ref, *refs):
    fixed, refs = refs[:3], refs[3:]
    quarter = lax.axis_index("pairs") * (total_ref.shape[0] // lax.axis_size("pairs"))
    for at, (shift, place) in enumerate(zip(shifts, places)):
        for block, tile in peer_tiles(shift, place, *fixed, *refs[3 * at : 3 * at + 3]):
            total_ref[block ^ quarter] += tile


def first_kernel(shifts, places, latent_ref, *refs):
    *refs, total_ref = refs
    ids_ref, _, coded_ref = refs[:3]
    total_ref[...] = jnp.zeros_like(total_ref)
    add_own(total_ref, ids_ref, latent_ref, coded_ref)
    add_peers(shifts, places, total_ref, *refs)


def middle_kernel(shifts, places, before_ref, *refs):
    *refs, total_ref = refs
    total_ref[...] = before_ref[...]
    add_peers(shifts, places, total_ref, *refs)


def last_kernel(shifts, places, before_ref, ids_ref, asked_ref, coded_ref, *refs):
    count = 3 * len(shifts)
    refs, part_refs = refs[:count], refs[count:]
    tiles = []
    for at, (shift, place) in enumerate(zip(shifts, places)):
        tiles += peer_tiles(shift, place, ids_ref, asked_ref, coded_ref, *refs[3 * at : 3 * at + 3])
    depth = part_refs[0].shape[0]
    quarter = lax.axis_index("pairs") * depth
    for place, part_ref in enumerate(part_refs):
        part_ref[...] = before_ref[place * depth : (place + 1) * depth]
        for block, tile in tiles:
            at = (block ^ quarter) - place * depth

            @pl.when((at >= 0) & (at < depth))
            def add():
                part_ref[at] += tile


def shift_groups(peers):
    top = peers // 2
    near = sorted(range(1, top), key=lambda at: (at.bit_length(), -at))
    return [[top]] + [[top + at, at] for at in near]


def estimate(slots, width, moved):
    return pl.CostEstimate(flops=12 * slots * width**3, bytes_accessed=moved, transcendentals=slots * width**2)


def swap(value, axis, shift):
    return lax.ppermute(value, axis, [(at, at ^ shift) for at in range(lax.axis_size(axis))])


def body(latent, left_block, right_block, slot_kind, edge_cols):
    tile, width = edge_cols.shape[-1], latent.shape[1]
    blocks = latent.reshape(-1, tile, width)
    peers, slots = left_block.shape[2:]
    lists = edge_cols.shape[4]

    def table(value):
        return value.reshape(peers, slots).T

    edges = edge_cols.reshape(peers, slots, lists, tile)
    top = peers // 2
    waited = pl.pallas_call(
        wait_kernel,
        out_shape=jax.ShapeDtypeStruct((8, 128), F32),
        out_specs=VMEM,
        compiler_params=PARAMS,
        cost_estimate=pl.CostEstimate(flops=WAIT_FLOPS, bytes_accessed=4096, transcendentals=0),
    )()
    blocks, ids, coded, far_coded = pl.pallas_call(
        setup_kernel,
        out_shape=(
            jax.ShapeDtypeStruct(blocks.shape, F32),
            jax.ShapeDtypeStruct((2, slots, peers), jnp.int32),
            jax.ShapeDtypeStruct(edges.shape, F32),
            jax.ShapeDtypeStruct((top, *edges.shape[1:]), F32),
        ),
        in_specs=[VMEM] * 4 + [HBM] * 2,
        out_specs=(VMEM,) * 4,
        scratch_shapes=[
            pltpu.VMEM(edges.shape, jnp.int32),
            pltpu.SemaphoreType.DMA((2,)),
        ],
        compiler_params=PARAMS,
    )(waited, table(left_block), table(right_block), table(slot_kind), blocks, edges)

    passed = swap(far_coded, "rows", top)
    near_message = jax.ShapeDtypeStruct((slots, tile + 2 * lists, width), F32)
    far_message = jax.ShapeDtypeStruct((slots, tile, width), F32)
    asked, where, leaving, arrived = right_block, [0], {}, {}
    for bit in [top] + [1 << at for at in range(top.bit_length() - 1)]:
        if len(where) == 1:
            asked = jnp.concatenate([ids[1:], table(swap(asked, "rows", bit))[None]])
        else:
            asked = jnp.concatenate([asked, swap(asked, "rows", bit)])
        where = where + [at ^ bit for at in where]
        shifts = sorted(where[len(where) // 2 :], reverse=True)
        sent = pl.pallas_call(
            functools.partial(pack_kernel, shifts, [where.index(at) for at in shifts]),
            out_shape=[far_message if at >= top else near_message for at in shifts],
            in_specs=[VMEM] * 5,
            out_specs=[VMEM] * len(shifts),
            compiler_params=PARAMS,
        )(ids, asked, blocks, coded, passed if bit < top else coded[:top])
        for shift, value in zip(shifts, sent):
            leaving[shift], arrived[shift] = value, swap(value, "rows", shift)

    whole = jax.ShapeDtypeStruct(blocks.shape, F32)
    parts = lax.axis_size("pairs")
    part = jax.ShapeDtypeStruct((blocks.shape[0] // parts, tile, width), F32)
    groups = shift_groups(peers)
    carrier = {at: passed if at == top else arrived[at % top] for at in arrived}
    total = [blocks]
    for group in groups:
        first, last = group is groups[0], group is groups[-1]
        messages = [value for at in group for value in (leaving[at], arrived[at], carrier[at])]
        total = pl.pallas_call(
            functools.partial(
                first_kernel if first else last_kernel if last else middle_kernel,
                group,
                [where.index(at) for at in group],
            ),
            out_shape=[part] * parts if last else [whole],
            in_specs=[VMEM] * (4 + len(messages)),
            out_specs=[VMEM] * (parts if last else 1),
            input_output_aliases={} if first or last else {0: 0},
            compiler_params=PARAMS,
            cost_estimate=estimate(slots * len(group), tile, 3 * blocks.size * 4),
        )(*total, ids, asked, coded, *messages)
    held = total
    far_half = held[2] + swap(held[3], "pairs", 1)
    kept = swap(held[1], "pairs", 1)
    result = held[0] + kept + swap(far_half, "pairs", 2)
    return result.reshape(-1, width)


def solution(mesh):
    return jax.shard_map(
        body,
        mesh=mesh,
        in_specs=(
            P("rows", None),
            P("rows", "pairs", None, None),
            P("rows", "pairs", None, None),
            P("rows", "pairs", None, None),
            P("rows", "pairs", None, None, None, None),
        ),
        out_specs=P(("rows", "pairs"), None),
        check_vma=False,
    )
```
